1024 devices in a mesh: row: 16 (over y, core), col: 64 (over z, x).
Axes of the slice: x: 4, y: 8, z: 16, core: 2. Of those that a mesh axis runs over, the one named last changes fastest.
Arguments:
- tangent: bfloat16 [16, 64, 64, 4096], P('row', 'col')
- block_row: int32 [16, 64, 64], P('row', 'col'), may hold values from 0 to 127
- block_col: int32 [16, 64, 64], P('row', 'col'), may hold values from 0 to 31
- tile_count: int32 [16, 64], P('row', 'col'), may hold values from 1 to 64, 2560 in all within a row
- old_basis: bfloat16 [2048, 3072], P(('row', 'col'))
- old_id: int32 [2048], P(('row', 'col')), may hold values from 0 to 2047, as said below
- residual: float32 [131072], P(('row', 'col'))
Outputs:
- recycled_c: bfloat16 [2048, 3072], P(('row', 'col'))
- recycled_u: bfloat16 [2048, 3072], P(('row', 'col'))
- coefficients: float32 [48], replicated
The draws below stay inside these ranges and needn't reach their ends.
Inputs may be any that keep to these rules, and one draw needn't show every extreme that they name: old_id is a permutation of the block rows. Write slot s = (128 * r + 2 * c + i) with 0 <= c < 64 and 0 <= i < 2, and p = i // 2. Its new block row is 128 * r + 2 * ((c + p + 1) mod (64)) + 2 * p + e, with e 0 or 1, the two slots of a pair taking different e. In each row of tile_count the largest count is exactly 64.
All inputs are finite; a program needn't handle non-finite values. No bound on the sum of `tile_count` on one device may be relied on, other than what follows from the above.
Results may differ from the reference program's by a relative error of at most 0.0012.
Values may be sent and summed in bfloat16 or wider, within the bound.
No kernel may reach another device: no remote copies, remote signals or barrier semaphores. Data moves between devices by JAX's collectives and lax.ppermute only.
A program may use at most 32 MiB of HBM per device.

```python
import math
import jax
import jax.numpy as jnp
import numpy as np
from jax import lax

BLK = 64
K = 48
RB_DEV = 2
NNZ = 64
NB = 2048
TR = 128
TC = 32
N_ROW = 16
N_COL = 64


def draw_tangent(key, part):
    row_groups = NB // TR
    col_groups = TR // RB_DEV
    shape = (row_groups, col_groups, NNZ, BLK, BLK)
    noise = jax.random.normal(jax.random.fold_in(key, 13), shape, jnp.float32)
    row_scale = jnp.exp(jax.random.uniform(jax.random.fold_in(key, 14), (row_groups, 1, 1, BLK, 1), jnp.float32, 0.0, math.log(10.0)))
    rising = jnp.exp(math.log(3.0) * jnp.arange(row_groups, dtype=jnp.float32) / max(row_groups - 1, 1))
    rising = rising.reshape(row_groups, 1, 1, 1, 1)
    per_row = NNZ / TR
    fan_scale = 1.0 / math.sqrt(16.0 * per_row * BLK * col_groups)
    values = noise * row_scale * rising * fan_scale
    return values.reshape(row_groups, col_groups, NNZ, BLK * BLK).astype(jnp.bfloat16)


def draw_old_basis(key, part):
    shape = (NB, BLK, K)
    col_scale = jnp.exp(jax.random.uniform(jax.random.fold_in(key, 21), (1, 1, K), jnp.float32, 0.0, math.log(10.0)))
    noise = jax.random.normal(jax.random.fold_in(key, 24), shape, jnp.float32)
    return (noise * col_scale).reshape(NB, BLK * K).astype(jnp.bfloat16)


def draw_old_id(key, part):
    row_groups = NB // TR
    col_groups = TR // RB_DEV
    pairs = RB_DEV // 2
    flips = jax.random.randint(jax.random.fold_in(key, 32), (row_groups, col_groups, pairs, 1), 0, 2)
    halves = jnp.arange(2, dtype=jnp.int32).reshape(1, 1, 1, 2)
    pair_ids = jnp.arange(pairs, dtype=jnp.int32).reshape(1, 1, pairs, 1)
    col_ids = jnp.arange(col_groups, dtype=jnp.int32).reshape(1, col_groups, 1, 1)
    dest_col = (col_ids + pair_ids + 1) % col_groups
    new_slot = 2 * pair_ids + (halves + flips) % 2
    group_ids = jnp.arange(row_groups, dtype=jnp.int32).reshape(row_groups, 1, 1, 1)
    ids = (group_ids * col_groups + dest_col) * RB_DEV + new_slot
    return ids.reshape(NB).astype(jnp.int32)


def draw_residual(key, part):
    total = NB * BLK
    position = jnp.arange(total, dtype=jnp.float32) / total
    rising = jnp.exp(math.log(3.0) * position)
    block_scale = jnp.exp(jax.random.uniform(jax.random.fold_in(key, 41), (NB, 1), jnp.float32, 0.0, math.log(10.0)))
    block_scale = jnp.broadcast_to(block_scale, (NB, BLK)).reshape(total)
    noise = jax.random.normal(jax.random.fold_in(key, 43), (total,), jnp.float32)
    return noise * rising * block_scale


def set_ends(array, own_key, least, high):
    longest = array.shape.index(max(array.shape))
    spots = []
    for shift in (0, 1):
        where = [jax.random.randint(jax.random.fold_in(own_key, axis), (), 0, length) for axis, length in enumerate(array.shape)]
        where[longest] = (where[longest] + shift) % array.shape[longest]
        spots.append(tuple(where))
    return array.at[spots[0]].set(least).at[spots[1]].set(high)


def profile(amount, total, reach, slope):
    portions = [(1 << 20) // math.isqrt(standing ** slope) + 1 for standing in range(2, amount + 1)]
    spare, given = total - reach - (amount - 1), [1] * (amount - 1)
    while spare > 0:
        candidates = [i for i in range(amount - 1) if given[i] < reach]
        pool, remaining = sum([portions[i] for i in candidates]), spare
        for i in candidates:
            more = min(reach - given[i], max(1, remaining * portions[i] // pool), spare)
            given[i] = given[i] + more
            spare = spare - more
    return np.array([reach] + given)


def ragged(own_key, number_of, total, limit, slope):
    if number_of == 2:
        one = jax.random.randint(own_key, (), max(1, total - limit), min(limit, total - 1) + 1)
        return jnp.stack([one, total - one])
    tallies = jnp.asarray(profile(number_of, total, limit, slope), jnp.int32)
    pairs = (number_of - 1) // 2
    source_of, receiver = tallies[1:1 + 2 * pairs:2], tallies[2:2 + 2 * pairs:2]
    room = jnp.minimum(source_of - 1, limit - receiver)
    shifted = jax.random.randint(jax.random.fold_in(own_key, 1), (pairs,), 0, 1 << 20) % (room + 1)
    tallies = tallies.at[1:1 + 2 * pairs:2].set(source_of - shifted).at[2:2 + 2 * pairs:2].set(receiver + shifted)
    return tallies[jax.random.permutation(jax.random.fold_in(own_key, 2), number_of)]


def setup_inputs(seed: int = 0) -> dict:
    splits = jax.random.split(jax.random.key(seed), 8)
    return {
        "tangent": draw_tangent(jax.random.fold_in(splits[7], 71), 0),
        "block_row": set_ends(jax.random.randint(splits[1], (N_ROW, N_COL, NNZ), 0, TR), jax.random.fold_in(splits[1], 1), 0, TR - 1).astype(jnp.int32),
        "block_col": set_ends(jax.random.randint(splits[2], (N_ROW, N_COL, NNZ), 0, TC), jax.random.fold_in(splits[2], 1), 0, TC - 1).astype(jnp.int32),
        "tile_count": jax.vmap(lambda own: ragged(own, N_COL, NNZ * 5 * N_COL // 8, NNZ, 2))(jax.random.split(splits[3], N_ROW)).reshape((N_ROW, N_COL)).astype(jnp.int32),
        "old_basis": draw_old_basis(jax.random.fold_in(splits[7], 71), 0),
        "old_id": draw_old_id(jax.random.fold_in(splits[7], 71), 0),
        "residual": draw_residual(jax.random.fold_in(splits[7], 71), 0),
    }


def reference(tangent, block_row, block_col, tile_count, old_basis, old_id, residual):
    highest = lax.Precision.HIGHEST
    basis = jnp.zeros_like(old_basis).at[old_id].set(old_basis)
    stacked = basis.reshape(NB, BLK, K)
    tiles = N_ROW * N_COL
    tile_ids = jnp.arange(tiles, dtype=jnp.int32)
    row_ids = tile_ids // N_COL
    col_ids = tile_ids % N_COL
    values = tangent.reshape(tiles, NNZ, BLK, BLK)
    rows_all = block_row.reshape(tiles, NNZ)
    cols_all = block_col.reshape(tiles, NNZ)
    counts = tile_count.reshape(tiles)

    def tile_step(carry, items):
        block_vals, local_rows, local_cols, live_count, row_idx, col_idx = items
        glob_rows = row_idx * TR + local_rows
        glob_cols = (local_cols // RB_DEV * N_COL + col_idx) * RB_DEV + local_cols % RB_DEV
        picked = stacked[glob_cols].astype(jnp.float32)
        prods = jnp.einsum('gij,gjk->gik', block_vals.astype(jnp.float32), picked, precision=highest)
        alive = jnp.arange(NNZ, dtype=jnp.int32) < live_count
        prods = jnp.where(alive[:, None, None], prods, jnp.float32(0.0))
        return (carry.at[glob_rows].add(prods), None)
    product, _ = lax.scan(tile_step, jnp.zeros((NB, BLK, K), jnp.float32), (values, rows_all, cols_all, counts, row_ids, col_ids))
    total_rows = NB * BLK
    flat_c = product.reshape(total_rows, K)
    gram = jnp.dot(flat_c.T, flat_c, precision=highest) / jnp.float32(total_rows)
    lower = jnp.linalg.cholesky(gram)
    ortho_t = jax.scipy.linalg.solve_triangular(lower, flat_c.T, lower=True)
    basis_t = jax.scipy.linalg.solve_triangular(lower, basis.astype(jnp.float32).reshape(total_rows, K).T, lower=True)
    coefficients = jnp.dot(ortho_t, residual, precision=highest) / jnp.float32(math.sqrt(total_rows))
    recycled_c = ortho_t.T.reshape(NB, BLK * K).astype(jnp.bfloat16)
    recycled_u = basis_t.T.reshape(NB, BLK * K).astype(jnp.bfloat16)
    return (recycled_c, recycled_u, coefficients)
```

```python
import math

import jax
import jax.numpy as jnp
from jax import lax
from jax.experimental import pallas as pl
from jax.experimental.pallas import tpu as pltpu
from jax.sharding import Mesh
from jax.sharding import PartitionSpec as P

BLK = 64
K = 48
PAIR = 2 * BLK
N_X, N_Y, N_Z, N_CORE = 4, 8, 16, 2
ROW = ("y", "core")
COL = ("z", "x")
N_ROW = N_Y * N_CORE
N_COL = N_Z * N_X
NNZ = 64
TOTAL = N_ROW * N_COL * PAIR
HIGHEST = lax.Precision.HIGHEST
VMEM = 48 * 1024 * 1024


def product_kernel(row_ref, col_ref, count_ref, tangent_ref, basis_ref, out_ref, half_ref):
    for q in range(N_ROW):
        half_ref[2 * q] = basis_ref[q, :, :BLK]
        half_ref[2 * q + 1] = basis_ref[q, :, BLK:]
    out_ref[...] = jnp.zeros_like(out_ref)
    count = count_ref[0]

    def add_block(n, carry):
        row = row_ref[n]
        owner = row >> 1
        place = (owner & (N_X - 1)) * N_Z + (owner >> 2)
        side = jnp.where(n < count, row & 1, 2)
        block = tangent_ref[n]
        none = jnp.zeros_like(block)
        sides = jnp.concatenate([jnp.where(side == 0, block, none), jnp.where(side == 1, block, none)], axis=0)
        out_ref[place] += lax.dot_general(
            half_ref[col_ref[n]], sides, (((1,), (1,)), ((), ())), preferred_element_type=jnp.float32
        )
        return carry

    lax.fori_loop(0, NNZ, add_block, 0, unroll=8)


def gram_kernel(parts_ref, residual_ref, product_ref, gram_ref):
    product = jnp.sum(parts_ref[...], axis=0)
    product_ref[...] = product
    first = lax.broadcasted_iota(jnp.int32, (16, PAIR), 0) == 0
    extra = jnp.where(first, jnp.broadcast_to(residual_ref[...], (16, PAIR)), 0.0)
    both = jnp.concatenate([product, extra], axis=0)
    gram = lax.dot_general(product, both, (((1,), (1,)), ((), ())), precision=HIGHEST)
    gram_ref[...] = jnp.concatenate([gram[: K // 2], gram[K // 2 :]], axis=1)


def finish_kernel(gram_ref, product_ref, basis_ref, out_c_ref, out_u_ref, coeff_ref):
    packed = gram_ref[...]
    upper = jnp.concatenate([packed[:, :BLK], packed[:, BLK:]], axis=0)
    work = jnp.concatenate([upper, jnp.zeros_like(upper)], axis=1)
    at_row = lax.broadcasted_iota(jnp.int32, (K, PAIR), 0)
    at_lane = lax.broadcasted_iota(jnp.int32, (K, PAIR), 1)
    work = jnp.where(at_lane < K, work * (1.0 / TOTAL), work)
    work = jnp.where(at_lane == at_row + BLK, 1.0, work)
    for k in range(K - 1):
        pivot_row = work[k : k + 1, :]
        factor = work[:, k : k + 1] / pivot_row[:, k : k + 1]
        work = work - jnp.where(at_row > k, factor * pivot_row, 0.0)
    pivots = jnp.sum(jnp.where(at_lane == at_row, work, 0.0), axis=1, keepdims=True)
    work = work / jnp.sqrt(pivots)
    inverse = jnp.where(at_lane >= BLK, work, 0.0)

    def transformed(columns):
        tall = jnp.concatenate(
            [jnp.zeros((BLK, PAIR), jnp.float32), columns, jnp.zeros((BLK - K, PAIR), jnp.float32)], axis=0
        )
        return jnp.dot(inverse, tall, precision=HIGHEST).T.astype(jnp.bfloat16)

    out_c_ref[...] = transformed(product_ref[...])
    out_u_ref[...] = transformed(basis_ref[...].astype(jnp.float32))
    inner = work[:, K : K + 1] * (1.0 / math.sqrt(TOTAL))
    coeff_ref[...] = jnp.sum(jnp.where(at_lane == at_row, inner, 0.0), axis=0, keepdims=True)


def summed(array, axes, count):
    copies = jnp.broadcast_to(array[None], (count,) + array.shape)
    return jnp.sum(lax.all_to_all(copies, axes, 0, 0, tiled=True), axis=0)


def per_device(tangent, block_row, block_col, tile_count, old_basis, old_id, residual):
    params = pltpu.CompilerParams(vmem_limit_bytes=VMEM)
    smem = pl.BlockSpec(memory_space=pltpu.SMEM)
    vmem = pl.BlockSpec(memory_space=pltpu.VMEM)
    ordered = jnp.where(old_id[0] % 2 == 0, old_basis, old_basis[::-1])
    sideways = ordered.reshape(2, BLK, K).transpose(2, 0, 1).reshape(K, PAIR)
    placed = lax.ppermute(sideways, COL, [(i, (i + 1) % N_COL) for i in range(N_COL)])
    copies = jnp.broadcast_to(placed[None], (N_ROW, K, PAIR))
    col_basis = lax.all_to_all(copies, ROW, 0, 0, tiled=True)
    partial = pl.pallas_call(
        product_kernel,
        out_shape=jax.ShapeDtypeStruct((N_COL, K, PAIR), jnp.float32),
        in_specs=[smem, smem, smem, vmem, vmem],
        out_specs=vmem,
        scratch_shapes=[pltpu.VMEM((2 * N_ROW, K, BLK), jnp.bfloat16)],
        compiler_params=params,
    )(block_row.reshape(NNZ), block_col.reshape(NNZ), tile_count.reshape(1), tangent.reshape(NNZ, BLK, BLK), col_basis)
    over_x = lax.all_to_all(partial, "x", 0, 0, tiled=True)
    over_x = jnp.sum(over_x.reshape(N_X, N_Z, K, PAIR), axis=0)
    over_z = lax.all_to_all(over_x, "z", 0, 0, tiled=True)
    product, gram = pl.pallas_call(
        gram_kernel,
        out_shape=(
            jax.ShapeDtypeStruct((K, PAIR), jnp.float32),
            jax.ShapeDtypeStruct((K // 2, PAIR), jnp.float32),
        ),
        in_specs=[vmem, vmem],
        out_specs=(vmem, vmem),
        compiler_params=params,
    )(over_z, residual.reshape(1, PAIR))
    gram = summed(gram, "x", N_X)
    gram = summed(gram, ROW, N_ROW)
    gram = summed(gram, "z", N_Z)
    out_c, out_u, coefficients = pl.pallas_call(
        finish_kernel,
        out_shape=(
            jax.ShapeDtypeStruct((PAIR, K), jnp.bfloat16),
            jax.ShapeDtypeStruct((PAIR, K), jnp.bfloat16),
            jax.ShapeDtypeStruct((1, PAIR), jnp.float32),
        ),
        in_specs=[vmem, vmem, vmem],
        out_specs=(vmem, vmem, vmem),
        compiler_params=params,
    )(gram, product, placed)
    return (out_c.reshape(2, BLK * K), out_u.reshape(2, BLK * K), coefficients[0, :K])


def solution(mesh):
    split = Mesh(mesh.devices.reshape(N_Y, N_CORE, N_Z, N_X), ("y", "core", "z", "x"))
    return jax.shard_map(
        per_device,
        mesh=split,
        in_specs=(
            P(ROW, COL, None, None),
            P(ROW, COL, None),
            P(ROW, COL, None),
            P(ROW, COL),
            P(ROW + COL, None),
            P(ROW + COL),
            P(ROW + COL),
        ),
        out_specs=(P(ROW + COL, None), P(ROW + COL, None), P()),
        check_vma=False,
    )
```

```python
import math

import jax
import jax.numpy as jnp
from jax import lax
from jax.experimental import pallas as pl
from jax.experimental.pallas import tpu as pltpu
from jax.sharding import Mesh
from jax.sharding import PartitionSpec as P

BLK = 64
K = 48
PAIR = 2 * BLK
N_X, N_Y, N_CORE = 4, 8, 2
N_Z_HI, N_Z_LO = 8, 2
ROW = ("y", "core")
NEAR = ("z_lo", "x")
COL = ("z_hi",) + NEAR
N_ROW = N_Y * N_CORE
N_NEAR = N_Z_LO * N_X
N_COL = N_Z_HI * N_NEAR
NNZ = 64
TOTAL = N_ROW * N_COL * PAIR
HIGHEST = lax.Precision.HIGHEST
VMEM = 48 * 1024 * 1024


def product_kernel(row_ref, col_ref, count_ref, tangent_ref, basis_ref, out_ref, half_ref):
    for q in range(N_ROW):
        half_ref[2 * q] = basis_ref[q, :, :BLK]
        half_ref[2 * q + 1] = basis_ref[q, :, BLK:]
    out_ref[...] = jnp.zeros_like(out_ref)
    count = count_ref[0]

    def add_block(n, carry):
        row = row_ref[n]
        owner = row >> 1
        place = (owner & (N_NEAR - 1)) * N_Z_HI + (owner >> 3)
        side = jnp.where(n < count, row & 1, 2)
        block = tangent_ref[n]
        none = jnp.zeros_like(block)
        sides = jnp.concatenate([jnp.where(side == 0, block, none), jnp.where(side == 1, block, none)], axis=0)
        out_ref[place] += lax.dot_general(
            half_ref[col_ref[n]], sides, (((1,), (1,)), ((), ())), preferred_element_type=jnp.float32
        )
        return carry

    lax.fori_loop(0, NNZ, add_block, 0, unroll=8)


def gram_kernel(parts_ref, residual_ref, product_ref, gram_ref):
    product = jnp.sum(parts_ref[...], axis=0)
    product_ref[...] = product
    first = lax.broadcasted_iota(jnp.int32, (16, PAIR), 0) == 0
    extra = jnp.where(first, jnp.broadcast_to(residual_ref[...], (16, PAIR)), 0.0)
    both = jnp.concatenate([product, extra], axis=0)
    gram = lax.dot_general(product, both, (((1,), (1,)), ((), ())), precision=HIGHEST)
    gram_ref[...] = jnp.concatenate([gram[: K // 2], gram[K // 2 :]], axis=1)


def finish_kernel(gram_ref, product_ref, basis_ref, out_c_ref, out_u_ref, coeff_ref):
    packed = gram_ref[...]
    upper = jnp.concatenate([packed[:, :BLK], packed[:, BLK:]], axis=0)
    work = jnp.concatenate([upper, jnp.zeros_like(upper)], axis=1)
    at_row = lax.broadcasted_iota(jnp.int32, (K, PAIR), 0)
    at_lane = lax.broadcasted_iota(jnp.int32, (K, PAIR), 1)
    work = jnp.where(at_lane < K, work * (1.0 / TOTAL), work)
    work = jnp.where(at_lane == at_row + BLK, 1.0, work)
    for k in range(K - 1):
        pivot_row = work[k : k + 1, :]
        factor = work[:, k : k + 1] / pivot_row[:, k : k + 1]
        work = work - jnp.where(at_row > k, factor * pivot_row, 0.0)
    pivots = jnp.sum(jnp.where(at_lane == at_row, work, 0.0), axis=1, keepdims=True)
    work = work / jnp.sqrt(pivots)
    inverse = jnp.where(at_lane >= BLK, work, 0.0)

    def transformed(columns):
        tall = jnp.concatenate(
            [jnp.zeros((BLK, PAIR), jnp.float32), columns, jnp.zeros((BLK - K, PAIR), jnp.float32)], axis=0
        )
        return jnp.dot(inverse, tall, precision=HIGHEST).T.astype(jnp.bfloat16)

    out_c_ref[...] = transformed(product_ref[...])
    out_u_ref[...] = transformed(basis_ref[...].astype(jnp.float32))
    inner = work[:, K : K + 1] * (1.0 / math.sqrt(TOTAL))
    coeff_ref[...] = jnp.sum(jnp.where(at_lane == at_row, inner, 0.0), axis=0)[:K]


def summed(array, axes, count):
    copies = jnp.broadcast_to(array[None], (count,) + array.shape)
    return jnp.sum(lax.all_to_all(copies, axes, 0, 0, tiled=True), axis=0)


def per_device(tangent, block_row, block_col, tile_count, old_basis, old_id, residual):
    params = pltpu.CompilerParams(vmem_limit_bytes=VMEM)
    smem = pl.BlockSpec(memory_space=pltpu.SMEM)
    vmem = pl.BlockSpec(memory_space=pltpu.VMEM)
    first, second = (old_basis[i].reshape(BLK, K).T for i in (0, 1))
    kept = old_id[0] % 2 == 0
    sideways = jnp.concatenate([jnp.where(kept, first, second), jnp.where(kept, second, first)], axis=1)
    placed = lax.ppermute(sideways, COL, [(i, (i + 1) % N_COL) for i in range(N_COL)])
    copies = jnp.broadcast_to(placed[None], (N_ROW, K, PAIR))
    col_basis = lax.all_to_all(copies, ROW, 0, 0, tiled=True)
    partial = pl.pallas_call(
        product_kernel,
        out_shape=jax.ShapeDtypeStruct((N_COL, K, PAIR), jnp.float32),
        in_specs=[smem, smem, smem, vmem, vmem],
        out_specs=vmem,
        scratch_shapes=[pltpu.VMEM((2 * N_ROW, K, BLK), jnp.bfloat16)],
        compiler_params=params,
    )(block_row.reshape(NNZ), block_col.reshape(NNZ), tile_count.reshape(1), tangent.reshape(NNZ, BLK, BLK), col_basis)
    near = lax.all_to_all(partial, NEAR, 0, 0, tiled=True)
    near = jnp.sum(near.reshape(N_NEAR, N_Z_HI, K, PAIR), axis=0)
    far = lax.all_to_all(near, "z_hi", 0, 0, tiled=True)
    product, gram = pl.pallas_call(
        gram_kernel,
        out_shape=(
            jax.ShapeDtypeStruct((K, PAIR), jnp.float32),
            jax.ShapeDtypeStruct((K // 2, PAIR), jnp.float32),
        ),
        in_specs=[vmem, vmem],
        out_specs=(vmem, vmem),
        compiler_params=params,
    )(far, residual.reshape(1, PAIR))
    gram = summed(gram, NEAR, N_NEAR)
    gram = summed(gram, ROW, N_ROW)
    gram = summed(gram, "z_hi", N_Z_HI)
    out_c, out_u, coefficients = pl.pallas_call(
        finish_kernel,
        out_shape=(
            jax.ShapeDtypeStruct((PAIR, K), jnp.bfloat16),
            jax.ShapeDtypeStruct((PAIR, K), jnp.bfloat16),
            jax.ShapeDtypeStruct((K,), jnp.float32),
        ),
        in_specs=[vmem, vmem, vmem],
        out_specs=(vmem, vmem, vmem),
        compiler_params=params,
    )(gram, product, placed)
    return (out_c.reshape(2, BLK * K), out_u.reshape(2, BLK * K), coefficients)


def solution(mesh):
    split = Mesh(mesh.devices.reshape(N_Y, N_CORE, N_Z_HI, N_Z_LO, N_X), ROW + COL)
    return jax.shard_map(
        per_device,
        mesh=split,
        in_specs=(
            P(ROW, COL, None, None),
            P(ROW, COL, None),
            P(ROW, COL, None),
            P(ROW, COL),
            P(ROW + COL, None),
            P(ROW + COL),
            P(ROW + COL),
        ),
        out_specs=(P(ROW + COL, None), P(ROW + COL, None), P()),
        check_vma=False,
    )
```

```python
import math

import jax
import jax.numpy as jnp
from jax import lax
from jax.experimental import pallas as pl
from jax.experimental.pallas import tpu as pltpu
from jax.sharding import Mesh
from jax.sharding import PartitionSpec as P

BLK = 64
K = 48
PAIR = 2 * BLK
N_X, N_Y, N_CORE = 4, 8, 2
N_Z_HI, N_Z_LO = 8, 2
ROW = ("y", "core")
NEAR = ("z_lo", "x")
COL = ("z_hi",) + NEAR
N_ROW = N_Y * N_CORE
N_NEAR = N_Z_LO * N_X
N_COL = N_Z_HI * N_NEAR
NNZ = 64
TOTAL = N_ROW * N_COL * PAIR
HIGHEST = lax.Precision.HIGHEST
VMEM = 48 * 1024 * 1024


HALF = BLK // 4
SHIFT = K
INNER = 2 * K
WORDS = 2 * HALF
STEPS = (64, 32, 16, 8, 4, 2, 1)
LOWEST = 100
MAGIC = 12582912.0


def encode(sums_ref, count, out_ref):
    def look(i, peak):
        return jnp.maximum(peak, jnp.abs(sums_ref[i]))

    peak = lax.fori_loop(0, count, look, jnp.zeros((K, PAIR), jnp.float32), unroll=8)
    peak = jnp.broadcast_to(jnp.max(peak, axis=1, keepdims=True), (K, PAIR))
    factor = jnp.full((K, PAIR), 2.0**19, jnp.float32)
    power = jnp.zeros((K, PAIR), jnp.int32)
    for step in STEPS:
        big = peak >= 2.0**step
        peak = jnp.where(big, peak * 2.0**-step, peak)
        factor = jnp.where(big, factor * 2.0**-step, factor)
        power = jnp.where(big, power + step, power)
    for step in STEPS:
        small = (peak < 2.0 ** (1 - step)) & (power - step >= -LOWEST)
        peak = jnp.where(small, peak * 2.0**step, peak)
        factor = jnp.where(small, factor * 2.0**step, factor)
        power = jnp.where(small, power - step, power)
    power = power + LOWEST
    lane = lax.broadcasted_iota(jnp.int32, (HALF, PAIR), 1)
    shown = jnp.where(lane < 8, power[:HALF], jnp.where(lane < 16, power[HALF:WORDS], power[WORDS:]))
    flags = ((shown >> (lane & 7)) & 1) << 10

    def put(i, carry):
        code = ((sums_ref[i] * factor + MAGIC) - MAGIC).astype(jnp.int32)
        code = jnp.minimum(code, (1 << 20) - 1)
        third = code[WORDS:]
        out_ref[i, :HALF] = (code[:HALF] << 11) | ((third >> 10) & 0x7FF)
        out_ref[i, HALF:] = (code[HALF:WORDS] << 11) | (third & 0x3FF) | flags
        return carry

    lax.fori_loop(0, count, put, 0, unroll=8)


def unit_of(second):
    lane = lax.broadcasted_iota(jnp.int32, (HALF, PAIR), 1)
    bits = (((second >> 10) & 1) << (lane & 7)).astype(jnp.float32)
    power = jnp.concatenate(
        [
            jnp.sum(jnp.where((lane >= 8 * i) & (lane < 8 * i + 8), bits, 0.0), axis=1, keepdims=True)
            for i in range(3)
        ],
        axis=0,
    )
    power = jnp.broadcast_to(power, (K, PAIR)).astype(jnp.int32)
    unit = jnp.full((K, PAIR), 2.0 ** (-LOWEST - 19), jnp.float32)
    for i in range(8):
        steps = (2.0 ** (1 << i),) if i < 7 else (2.0**64, 2.0**64)
        for step in steps:
            unit = jnp.where(((power >> i) & 1) == 1, unit * step, unit)
    return unit


def decode(words):
    first, second = words[:HALF], words[HALF:]
    third = ((first << 21) >> 11) | (second & 0x3FF)
    return jnp.concatenate([first >> 11, second >> 11, third], axis=0).astype(jnp.float32)


def near_kernel(near_ref, out_ref, unit_ref, sums_ref):
    for source in range(N_NEAR):
        unit_ref[source] = unit_of(near_ref[source, 0, HALF:])

    def add(i, carry):
        total = decode(near_ref[0, i]) * unit_ref[0]
        for source in range(1, N_NEAR):
            total += decode(near_ref[source, i]) * unit_ref[source]
        sums_ref[i] = total
        return carry

    lax.fori_loop(0, N_Z_HI, add, 0)
    encode(sums_ref, N_Z_HI, out_ref)


def product_kernel(row_ref, col_ref, count_ref, tangent_ref, basis_ref, out_ref, half_ref, sums_ref):
    for q in range(N_ROW):
        half_ref[2 * q] = basis_ref[q, :, :BLK]
        half_ref[2 * q + 1] = basis_ref[q, :, BLK:]
    sums_ref[...] = jnp.zeros_like(sums_ref)
    count = count_ref[0]

    def add_block(n, carry):
        row = row_ref[n]
        owner = row >> 1
        place = (owner & (N_NEAR - 1)) * N_Z_HI + (owner >> 3)
        side = jnp.where(n < count, row & 1, 2)
        block = tangent_ref[n]
        none = jnp.zeros_like(block)
        sides = jnp.concatenate([jnp.where(side == 0, block, none), jnp.where(side == 1, block, none)], axis=0)
        sums_ref[place] += lax.dot_general(
            half_ref[col_ref[n]], sides, (((1,), (1,)), ((), ())), preferred_element_type=jnp.float32
        )
        return carry

    lax.fori_loop(0, NNZ, add_block, 0, unroll=8)
    encode(sums_ref, N_COL, out_ref)


def gram_kernel(far_ref, residual_ref, product_ref, gram_ref):
    product = decode(far_ref[0]) * unit_of(far_ref[0, HALF:])
    for source in range(1, N_Z_HI):
        product += decode(far_ref[source]) * unit_of(far_ref[source, HALF:])
    product_ref[...] = product
    at_row = lax.broadcasted_iota(jnp.int32, (PAIR - K, PAIR), 0)
    extra = jnp.where((at_row == 1) | (at_row == K), residual_ref[...], 0.0)
    both = jnp.concatenate([product, extra], axis=0)
    gram = lax.dot_general(product, both, (((1,), (1,)), ((), ())), precision=HIGHEST)
    lane = lax.broadcasted_iota(jnp.int32, (HALF, PAIR), 1)
    top, middle, bottom = gram[:HALF], gram[HALF:WORDS], gram[WORDS:]
    gram_ref[...] = jnp.where(
        (lane < K) | (lane == 96),
        bottom,
        jnp.where((lane < 80) | (lane == 97), pltpu.roll(middle, 48, 1), pltpu.roll(top, 112, 1)),
    )


def finish_kernel(gram_ref, product_ref, basis_ref, out_c_ref, out_u_ref, coeff_ref):
    packed = gram_ref[...]
    top = pltpu.roll(packed, 16, 1)
    blocks = jnp.concatenate([top, pltpu.roll(packed, 80, 1), packed], axis=0)
    inner = jnp.concatenate([top, pltpu.roll(packed, 127, 1), packed], axis=0)
    at_row = lax.broadcasted_iota(jnp.int32, (K, PAIR), 0)
    at_lane = lax.broadcasted_iota(jnp.int32, (K, PAIR), 1)
    blocks = blocks * (1.0 / TOTAL)
    below = jnp.concatenate([jnp.where(at_lane < at_row, blocks, 0.0), jnp.zeros((PAIR - K, PAIR), jnp.float32)], axis=0)
    work = jnp.where(at_lane <= at_row, blocks, below.T[:K])
    work = jnp.where(at_lane == INNER, inner, work)
    work = jnp.where(at_lane == at_row + SHIFT, 1.0, work)
    for k in range(K - 1):
        pivot_row = work[k : k + 1, :]
        factor = work[:, k : k + 1] / pivot_row[:, k : k + 1]
        work = work - jnp.where(at_row > k, factor * pivot_row, 0.0)
    pivots = jnp.sum(jnp.where(at_lane == at_row, work, 0.0), axis=1, keepdims=True)
    work = work / jnp.sqrt(pivots)
    inverse = jnp.where((at_lane >= SHIFT) & (at_lane < INNER), work, 0.0)

    def transformed(columns):
        tall = jnp.concatenate(
            [jnp.zeros((SHIFT, PAIR), jnp.float32), columns, jnp.zeros((PAIR - INNER, PAIR), jnp.float32)], axis=0
        )
        return jnp.dot(inverse, tall, precision=HIGHEST).T.astype(jnp.bfloat16)

    out_c_ref[...] = transformed(product_ref[...])
    out_u_ref[...] = transformed(basis_ref[...].astype(jnp.float32))
    inner = work[:, INNER : INNER + 1] * (1.0 / math.sqrt(TOTAL))
    coeff_ref[...] = jnp.sum(jnp.where(at_lane == at_row, inner, 0.0), axis=0)[:K]


def summed(array, axes, count):
    copies = jnp.broadcast_to(array[None], (count,) + array.shape)
    return jnp.sum(lax.all_to_all(copies, axes, 0, 0, tiled=True), axis=0)


def per_device(tangent, block_row, block_col, tile_count, old_basis, old_id, residual):
    params = pltpu.CompilerParams(vmem_limit_bytes=VMEM)
    smem = pl.BlockSpec(memory_space=pltpu.SMEM)
    vmem = pl.BlockSpec(memory_space=pltpu.VMEM)
    first, second = (old_basis[i].reshape(BLK, K).T for i in (0, 1))
    kept = old_id[0] % 2 == 0
    sideways = jnp.concatenate([jnp.where(kept, first, second), jnp.where(kept, second, first)], axis=1)
    placed = lax.ppermute(sideways, COL, [(i, (i + 1) % N_COL) for i in range(N_COL)])
    blocks, sent = lax.optimization_barrier((tangent.reshape(NNZ, BLK, BLK), placed))
    copies = jnp.broadcast_to(sent[None], (N_ROW, K, PAIR))
    col_basis = lax.all_to_all(copies, ROW, 0, 0, tiled=True)
    partial = pl.pallas_call(
        product_kernel,
        out_shape=jax.ShapeDtypeStruct((N_COL, WORDS, PAIR), jnp.int32),
        in_specs=[smem, smem, smem, vmem, vmem],
        out_specs=vmem,
        scratch_shapes=[pltpu.VMEM((2 * N_ROW, K, BLK), jnp.bfloat16), pltpu.VMEM((N_COL, K, PAIR), jnp.float32)],
        compiler_params=params,
    )(block_row.reshape(NNZ), block_col.reshape(NNZ), tile_count.reshape(1), blocks, col_basis)
    near = lax.all_to_all(partial, NEAR, 0, 0, tiled=True)
    near = pl.pallas_call(
        near_kernel,
        out_shape=jax.ShapeDtypeStruct((N_Z_HI, WORDS, PAIR), jnp.int32),
        in_specs=[vmem],
        out_specs=vmem,
        scratch_shapes=[pltpu.VMEM((N_NEAR, K, PAIR), jnp.float32), pltpu.VMEM((N_Z_HI, K, PAIR), jnp.float32)],
        compiler_params=params,
    )(near.reshape(N_NEAR, N_Z_HI, WORDS, PAIR))
    far = lax.all_to_all(near, "z_hi", 0, 0, tiled=True)
    product, gram = pl.pallas_call(
        gram_kernel,
        out_shape=(
            jax.ShapeDtypeStruct((K, PAIR), jnp.float32),
            jax.ShapeDtypeStruct((HALF, PAIR), jnp.float32),
        ),
        in_specs=[vmem, vmem],
        out_specs=(vmem, vmem),
        compiler_params=params,
    )(far, residual.reshape(1, PAIR))
    gram = summed(gram, NEAR, N_NEAR)
    gram = summed(gram, ROW, N_ROW)
    gram = summed(gram, "z_hi", N_Z_HI)
    out_c, out_u, coefficients = pl.pallas_call(
        finish_kernel,
        out_shape=(
            jax.ShapeDtypeStruct((PAIR, K), jnp.bfloat16),
            jax.ShapeDtypeStruct((PAIR, K), jnp.bfloat16),
            jax.ShapeDtypeStruct((K,), jnp.float32),
        ),
        in_specs=[vmem, vmem, vmem],
        out_specs=(vmem, vmem, vmem),
        compiler_params=params,
    )(gram, product, placed)
    return (out_c.reshape(2, BLK * K), out_u.reshape(2, BLK * K), coefficients)


def solution(mesh):
    split = Mesh(mesh.devices.reshape(N_Y, N_CORE, N_Z_HI, N_Z_LO, N_X), ROW + COL)
    return jax.shard_map(
        per_device,
        mesh=split,
        in_specs=(
            P(ROW, COL, None, None),
            P(ROW, COL, None),
            P(ROW, COL, None),
            P(ROW, COL),
            P(ROW + COL, None),
            P(ROW + COL),
            P(ROW + COL),
        ),
        out_specs=(P(ROW + COL, None), P(ROW + COL, None), P()),
        check_vma=False,
    )
```

```python
import math

import jax
import jax.numpy as jnp
from jax import lax
from jax.experimental import pallas as pl
from jax.experimental.pallas import tpu as pltpu
from jax.sharding import Mesh
from jax.sharding import PartitionSpec as P

BLK = 64
K = 48
PAIR = 2 * BLK
N_X, N_Y, N_CORE = 4, 8, 2
N_Z_HI, N_Z_LO = 8, 2
ROW = ("y", "core")
NEAR = ("z_lo", "x")
COL = ("z_hi",) + NEAR
N_ROW = N_Y * N_CORE
N_NEAR = N_Z_LO * N_X
N_COL = N_Z_HI * N_NEAR
NNZ = 64
TOTAL = N_ROW * N_COL * PAIR
HIGHEST = lax.Precision.HIGHEST
VMEM = 48 * 1024 * 1024


HALF = BLK // 4
SHIFT = K
INNER = 2 * K
WORDS = 2 * HALF
STEPS = (64, 32, 16, 8, 4, 2, 1)
LOWEST = 100
MAGIC = 12582912.0


def encode(sums_ref, count, out_ref):
    def look(i, peak):
        return jnp.maximum(peak, jnp.abs(sums_ref[i]))

    peak = lax.fori_loop(0, count, look, jnp.zeros((K, PAIR), jnp.float32), unroll=8)
    peak = jnp.broadcast_to(jnp.max(peak, axis=1, keepdims=True), (K, PAIR))
    factor = jnp.full((K, PAIR), 2.0**19, jnp.float32)
    power = jnp.zeros((K, PAIR), jnp.int32)
    for step in STEPS:
        big = peak >= 2.0**step
        peak = jnp.where(big, peak * 2.0**-step, peak)
        factor = jnp.where(big, factor * 2.0**-step, factor)
        power = jnp.where(big, power + step, power)
    for step in STEPS:
        small = (peak < 2.0 ** (1 - step)) & (power - step >= -LOWEST)
        peak = jnp.where(small, peak * 2.0**step, peak)
        factor = jnp.where(small, factor * 2.0**step, factor)
        power = jnp.where(small, power - step, power)
    power = power + LOWEST
    lane = lax.broadcasted_iota(jnp.int32, (HALF, PAIR), 1)
    shown = jnp.where(lane < 8, power[:HALF], jnp.where(lane < 16, power[HALF:WORDS], power[WORDS:]))
    flags = ((shown >> (lane & 7)) & 1) << 10

    def put(i, carry):
        code = ((sums_ref[i] * factor + MAGIC) - MAGIC).astype(jnp.int32)
        code = jnp.minimum(code, (1 << 20) - 1)
        third = code[WORDS:]
        out_ref[i, :HALF] = (code[:HALF] << 11) | ((third >> 10) & 0x7FF)
        out_ref[i, HALF:] = (code[HALF:WORDS] << 11) | (third & 0x3FF) | flags
        return carry

    lax.fori_loop(0, count, put, 0, unroll=8)


def unit_of(second):
    lane = lax.broadcasted_iota(jnp.int32, (HALF, PAIR), 1)
    bits = (((second >> 10) & 1) << (lane & 7)).astype(jnp.float32)
    power = jnp.concatenate(
        [
            jnp.sum(jnp.where((lane >= 8 * i) & (lane < 8 * i + 8), bits, 0.0), axis=1, keepdims=True)
            for i in range(3)
        ],
        axis=0,
    )
    power = jnp.broadcast_to(power, (K, PAIR)).astype(jnp.int32)
    unit = jnp.full((K, PAIR), 2.0 ** (-LOWEST - 19), jnp.float32)
    for i in range(8):
        steps = (2.0 ** (1 << i),) if i < 7 else (2.0**64, 2.0**64)
        for step in steps:
            unit = jnp.where(((power >> i) & 1) == 1, unit * step, unit)
    return unit


def decode(words):
    first, second = words[:HALF], words[HALF:]
    third = ((first << 21) >> 11) | (second & 0x3FF)
    return jnp.concatenate([first >> 11, second >> 11, third], axis=0).astype(jnp.float32)


def near_kernel(near_ref, out_ref, unit_ref, sums_ref):
    for source in range(N_NEAR):
        unit_ref[source] = unit_of(near_ref[source, 0, HALF:])

    def add(i, carry):
        total = decode(near_ref[0, i]) * unit_ref[0]
        for source in range(1, N_NEAR):
            total += decode(near_ref[source, i]) * unit_ref[source]
        sums_ref[i] = total
        return carry

    lax.fori_loop(0, N_Z_HI, add, 0)
    encode(sums_ref, N_Z_HI, out_ref)


def product_kernel(slot_ref, tangent_ref, basis_ref, out_ref, half_ref, sums_ref):
    for q in range(N_ROW):
        half_ref[2 * q] = basis_ref[q, :, :BLK]
        half_ref[2 * q + 1] = basis_ref[q, :, BLK:]
    sums_ref[...] = jnp.zeros_like(sums_ref)

    def add_block(n, carry):
        slot = slot_ref[n]
        place = slot & (N_COL - 1)
        side = (slot >> 6) & 3
        block = tangent_ref[n]
        none = jnp.zeros_like(block)
        sides = jnp.concatenate([jnp.where(side == 0, block, none), jnp.where(side == 1, block, none)], axis=0)
        sums_ref[place] += lax.dot_general(
            half_ref[slot >> 8], sides, (((1,), (1,)), ((), ())), preferred_element_type=jnp.float32
        )
        return carry

    lax.fori_loop(0, NNZ, add_block, 0, unroll=8)
    encode(sums_ref, N_COL, out_ref)


def gram_kernel(far_ref, extra_ref, product_ref, gram_ref):
    product = decode(far_ref[0]) * unit_of(far_ref[0, HALF:])
    for source in range(1, N_Z_HI):
        product += decode(far_ref[source]) * unit_of(far_ref[source, HALF:])
    product_ref[...] = product
    both = jnp.concatenate([product, extra_ref[...]], axis=0)
    gram = lax.dot_general(product, both, (((1,), (1,)), ((), ())), precision=HIGHEST)
    lane = lax.broadcasted_iota(jnp.int32, (HALF, PAIR), 1)
    top, middle, bottom = gram[:HALF], gram[HALF:WORDS], gram[WORDS:]
    gram_ref[...] = jnp.where(
        (lane < K) | (lane == 96),
        bottom,
        jnp.where((lane < 80) | (lane == 97), pltpu.roll(middle, 48, 1), pltpu.roll(top, 112, 1)),
    )


def finish_kernel(gram_ref, product_ref, basis_ref, out_c_ref, out_u_ref, coeff_ref):
    packed = gram_ref[...]
    top = pltpu.roll(packed, 16, 1)
    blocks = jnp.concatenate([top, pltpu.roll(packed, 80, 1), packed], axis=0)
    inner = jnp.concatenate([top, pltpu.roll(packed, 127, 1), packed], axis=0)
    at_row = lax.broadcasted_iota(jnp.int32, (K, PAIR), 0)
    at_lane = lax.broadcasted_iota(jnp.int32, (K, PAIR), 1)
    blocks = blocks * (1.0 / TOTAL)
    below = jnp.concatenate([jnp.where(at_lane < at_row, blocks, 0.0), jnp.zeros((PAIR - K, PAIR), jnp.float32)], axis=0)
    work = jnp.where(at_lane <= at_row, blocks, below.T[:K])
    work = jnp.where(at_lane == INNER, inner, work)
    work = jnp.where(at_lane == at_row + SHIFT, 1.0, work)
    for k in range(K - 1):
        pivot_row = work[k : k + 1, :]
        factor = work[:, k : k + 1] / pivot_row[:, k : k + 1]
        work = work - jnp.where(at_row > k, factor * pivot_row, 0.0)
    pivots = jnp.sum(jnp.where(at_lane == at_row, work, 0.0), axis=1, keepdims=True)
    work = work / jnp.sqrt(pivots)
    inverse = jnp.where((at_lane >= SHIFT) & (at_lane < INNER), work, 0.0)

    def transformed(columns):
        tall = jnp.concatenate(
            [jnp.zeros((SHIFT, PAIR), jnp.float32), columns, jnp.zeros((PAIR - INNER, PAIR), jnp.float32)], axis=0
        )
        return jnp.dot(inverse, tall, precision=HIGHEST).T.astype(jnp.bfloat16)

    out_c_ref[...] = transformed(product_ref[...])
    out_u_ref[...] = transformed(basis_ref[...].astype(jnp.float32))
    inner = work[:, INNER : INNER + 1] * (1.0 / math.sqrt(TOTAL))
    coeff_ref[...] = jnp.sum(jnp.where(at_lane == at_row, inner, 0.0), axis=0)[:K]


def summed(array, axes, count):
    copies = jnp.broadcast_to(array[None], (count,) + array.shape)
    return jnp.sum(lax.all_to_all(copies, axes, 0, 0, tiled=True), axis=0)


def per_device(tangent, block_row, block_col, tile_count, old_basis, old_id, residual):
    params = pltpu.CompilerParams(vmem_limit_bytes=VMEM)
    smem = pl.BlockSpec(memory_space=pltpu.SMEM)
    vmem = pl.BlockSpec(memory_space=pltpu.VMEM)
    first, second = (old_basis[i].reshape(BLK, K).T for i in (0, 1))
    kept = old_id[0] % 2 == 0
    sideways = jnp.concatenate([jnp.where(kept, first, second), jnp.where(kept, second, first)], axis=1)
    placed = lax.ppermute(sideways, COL, [(i, (i + 1) % N_COL) for i in range(N_COL)])
    rows, cols = block_row.reshape(NNZ), block_col.reshape(NNZ)
    owner = rows >> 1
    side = jnp.where(jnp.arange(NNZ) < tile_count.reshape(1), rows & 1, 2)
    slots = (owner & (N_NEAR - 1)) * N_Z_HI + (owner >> 3) + (side << 6) + (cols << 8)
    at_row = lax.broadcasted_iota(jnp.int32, (PAIR - K, PAIR), 0)
    extra = jnp.where((at_row == 1) | (at_row == K), residual.reshape(1, PAIR), 0.0)
    blocks, slots, extra, sent = lax.optimization_barrier((tangent.reshape(NNZ, BLK, BLK), slots, extra, placed))
    copies = jnp.broadcast_to(sent[None], (N_ROW, K, PAIR))
    col_basis = lax.all_to_all(copies, ROW, 0, 0, tiled=True)
    partial = pl.pallas_call(
        product_kernel,
        out_shape=jax.ShapeDtypeStruct((N_COL, WORDS, PAIR), jnp.int32),
        in_specs=[smem, vmem, vmem],
        out_specs=vmem,
        scratch_shapes=[pltpu.VMEM((2 * N_ROW, K, BLK), jnp.bfloat16), pltpu.VMEM((N_COL, K, PAIR), jnp.float32)],
        compiler_params=params,
    )(slots, blocks, col_basis)
    near = lax.all_to_all(partial, NEAR, 0, 0, tiled=True)
    near = pl.pallas_call(
        near_kernel,
        out_shape=jax.ShapeDtypeStruct((N_Z_HI, WORDS, PAIR), jnp.int32),
        in_specs=[vmem],
        out_specs=vmem,
        scratch_shapes=[pltpu.VMEM((N_NEAR, K, PAIR), jnp.float32), pltpu.VMEM((N_Z_HI, K, PAIR), jnp.float32)],
        compiler_params=params,
    )(near.reshape(N_NEAR, N_Z_HI, WORDS, PAIR))
    far = lax.all_to_all(near, "z_hi", 0, 0, tiled=True)
    product, gram = pl.pallas_call(
        gram_kernel,
        out_shape=(
            jax.ShapeDtypeStruct((K, PAIR), jnp.float32),
            jax.ShapeDtypeStruct((HALF, PAIR), jnp.float32),
        ),
        in_specs=[vmem, vmem],
        out_specs=(vmem, vmem),
        compiler_params=params,
    )(far, extra)
    gram = summed(gram, NEAR, N_NEAR)
    gram = summed(gram, ROW, N_ROW)
    gram = summed(gram, "z_hi", N_Z_HI)
    out_c, out_u, coefficients = pl.pallas_call(
        finish_kernel,
        out_shape=(
            jax.ShapeDtypeStruct((PAIR, K), jnp.bfloat16),
            jax.ShapeDtypeStruct((PAIR, K), jnp.bfloat16),
            jax.ShapeDtypeStruct((K,), jnp.float32),
        ),
        in_specs=[vmem, vmem, vmem],
        out_specs=(vmem, vmem, vmem),
        compiler_params=params,
    )(gram, product, placed)
    return (out_c.reshape(2, BLK * K), out_u.reshape(2, BLK * K), coefficients)


def solution(mesh):
    split = Mesh(mesh.devices.reshape(N_Y, N_CORE, N_Z_HI, N_Z_LO, N_X), ROW + COL)
    return jax.shard_map(
        per_device,
        mesh=split,
        in_specs=(
            P(ROW, COL, None, None),
            P(ROW, COL, None),
            P(ROW, COL, None),
            P(ROW, COL),
            P(ROW + COL, None),
            P(ROW + COL),
            P(ROW + COL),
        ),
        out_specs=(P(ROW + COL, None), P(ROW + COL, None), P()),
        check_vma=False,
    )
```

```python
import math

import jax
import jax.numpy as jnp
from jax import lax
from jax.experimental import pallas as pl
from jax.experimental.pallas import tpu as pltpu
from jax.sharding import Mesh
from jax.sharding import PartitionSpec as P

BLK = 64
K = 48
PAIR = 2 * BLK
N_X, N_Y, N_CORE = 4, 8, 2
N_Z_HI, N_Z_LO = 8, 2
ROW = ("y", "core")
NEAR = ("z_lo", "x")
COL = ("z_hi",) + NEAR
N_ROW = N_Y * N_CORE
N_NEAR = N_Z_LO * N_X
N_COL = N_Z_HI * N_NEAR
NNZ = 64
TOTAL = N_ROW * N_COL * PAIR
HIGHEST = lax.Precision.HIGHEST
VMEM = 48 * 1024 * 1024


HALF = BLK // 4
PANEL = 8
BATCH = 8
SHIFT = K
INNER = 2 * K
WORDS = 2 * HALF
STEPS = (64, 32, 16, 8, 4, 2, 1)
LOWEST = 100
MAGIC = 12582912.0


def encode(sums_ref, count, out_ref):
    def look(i, peak):
        return jnp.maximum(peak, jnp.abs(sums_ref[i]))

    peak = lax.fori_loop(0, count, look, jnp.zeros((K, PAIR), jnp.float32), unroll=8)
    peak = jnp.broadcast_to(jnp.max(peak, axis=1, keepdims=True), (K, PAIR))
    factor = jnp.full((K, PAIR), 2.0**19, jnp.float32)
    power = jnp.zeros((K, PAIR), jnp.int32)
    for step in STEPS:
        big = peak >= 2.0**step
        peak = jnp.where(big, peak * 2.0**-step, peak)
        factor = jnp.where(big, factor * 2.0**-step, factor)
        power = jnp.where(big, power + step, power)
    for step in STEPS:
        small = (peak < 2.0 ** (1 - step)) & (power - step >= -LOWEST)
        peak = jnp.where(small, peak * 2.0**step, peak)
        factor = jnp.where(small, factor * 2.0**step, factor)
        power = jnp.where(small, power - step, power)
    power = power + LOWEST
    lane = lax.broadcasted_iota(jnp.int32, (HALF, PAIR), 1)
    shown = jnp.where(lane < 8, power[:HALF], jnp.where(lane < 16, power[HALF:WORDS], power[WORDS:]))
    flags = ((shown >> (lane & 7)) & 1) << 10

    def put(i, carry):
        code = ((sums_ref[i] * factor + MAGIC) - MAGIC).astype(jnp.int32)
        code = jnp.minimum(code, (1 << 20) - 1)
        third = code[WORDS:]
        out_ref[i, :HALF] = (code[:HALF] << 11) | ((third >> 10) & 0x7FF)
        out_ref[i, HALF:] = (code[HALF:WORDS] << 11) | (third & 0x3FF) | flags
        return carry

    lax.fori_loop(0, count, put, 0, unroll=8)


def unit_of(second):
    lane = lax.broadcasted_iota(jnp.int32, (HALF, PAIR), 1)
    bits = (((second >> 10) & 1) << (lane & 7)).astype(jnp.float32)
    power = jnp.concatenate(
        [
            jnp.sum(jnp.where((lane >= 8 * i) & (lane < 8 * i + 8), bits, 0.0), axis=1, keepdims=True)
            for i in range(3)
        ],
        axis=0,
    )
    power = jnp.broadcast_to(power, (K, PAIR)).astype(jnp.int32)
    unit = jnp.full((K, PAIR), 2.0 ** (-LOWEST - 19), jnp.float32)
    for i in range(8):
        steps = (2.0 ** (1 << i),) if i < 7 else (2.0**64, 2.0**64)
        for step in steps:
            unit = jnp.where(((power >> i) & 1) == 1, unit * step, unit)
    return unit


def decode(words):
    first, second = words[:HALF], words[HALF:]
    third = ((first << 21) >> 11) | (second & 0x3FF)
    return jnp.concatenate([first >> 11, second >> 11, third], axis=0).astype(jnp.float32)


def near_kernel(near_ref, out_ref, unit_ref, sums_ref):
    for source in range(N_NEAR):
        unit_ref[source] = unit_of(near_ref[source, 0, HALF:])

    def add(i, carry):
        total = decode(near_ref[0, i]) * unit_ref[0]
        for source in range(1, N_NEAR):
            total += decode(near_ref[source, i]) * unit_ref[source]
        sums_ref[i] = total
        return carry

    lax.fori_loop(0, N_Z_HI, add, 0)
    encode(sums_ref, N_Z_HI, out_ref)


def product_kernel(slot_ref, tangent_ref, basis_ref, out_ref, half_ref, sums_ref):
    for q in range(N_ROW):
        half_ref[2 * q] = basis_ref[q, :, :BLK]
        half_ref[2 * q + 1] = basis_ref[q, :, BLK:]
    sums_ref[...] = jnp.zeros_like(sums_ref)

    def add_blocks(step, carry):
        places, products = [], []
        for i in range(BATCH):
            n = step * BATCH + i
            slot = slot_ref[n]
            places.append(slot & (N_COL - 1))
            side = (slot >> 6) & 3
            block = tangent_ref[n]
            none = jnp.zeros_like(block)
            sides = jnp.concatenate([jnp.where(side == 0, block, none), jnp.where(side == 1, block, none)], axis=0)
            products.append(
                lax.dot_general(
                    half_ref[slot >> 8], sides, (((1,), (1,)), ((), ())), preferred_element_type=jnp.float32
                )
            )
        for place, product in zip(places, products):
            sums_ref[place] += product
        return carry

    lax.fori_loop(0, NNZ // BATCH, add_blocks, 0)
    encode(sums_ref, N_COL, out_ref)


def gram_kernel(far_ref, extra_ref, product_ref, gram_ref):
    product = decode(far_ref[0]) * unit_of(far_ref[0, HALF:])
    for source in range(1, N_Z_HI):
        product += decode(far_ref[source]) * unit_of(far_ref[source, HALF:])
    product_ref[...] = product
    both = jnp.concatenate([product, extra_ref[...]], axis=0)
    gram = lax.dot_general(product, both, (((1,), (1,)), ((), ())), precision=HIGHEST)
    lane = lax.broadcasted_iota(jnp.int32, (HALF, PAIR), 1)
    top, middle, bottom = gram[:HALF], gram[HALF:WORDS], gram[WORDS:]
    gram_ref[...] = jnp.where(
        (lane < K) | (lane == 96),
        bottom,
        jnp.where((lane < 80) | (lane == 97), pltpu.roll(middle, 48, 1), pltpu.roll(top, 112, 1)),
    )


def finish_kernel(gram_ref, product_ref, basis_ref, out_c_ref, out_u_ref, coeff_ref, both_ref):
    packed = gram_ref[...]
    top = pltpu.roll(packed, 16, 1)
    blocks = jnp.concatenate([top, pltpu.roll(packed, 80, 1), packed], axis=0)
    inner = jnp.concatenate([top, pltpu.roll(packed, 127, 1), packed], axis=0)
    at_row = lax.broadcasted_iota(jnp.int32, (K, PAIR), 0)
    at_lane = lax.broadcasted_iota(jnp.int32, (K, PAIR), 1)
    blocks = blocks * (1.0 / TOTAL)
    below = jnp.concatenate([jnp.where(at_lane < at_row, blocks, 0.0), jnp.zeros((PAIR - K, PAIR), jnp.float32)], axis=0)
    work = jnp.where(at_lane <= at_row, blocks, below.T[:K])
    work = jnp.where(at_lane == INNER, inner, work)
    work = jnp.where(at_lane == at_row + SHIFT, 1.0, work)
    groups = [work[i : i + 8] for i in range(0, K, 8)]
    in_group = at_row[:8]
    pivots = [jnp.ones((8, PAIR), jnp.float32)] * len(groups)
    for start in range(0, K, PANEL):
        own = start // 8
        first = start % 8
        columns = [
            [jnp.broadcast_to(group[:, k : k + 1], (8, PAIR)) for group in groups[own:]]
            for k in range(start, start + PANEL)
        ]
        rows = [groups[own][first + i : first + i + 1] for i in range(PANEL)]
        for i in range(PANEL):
            pivot = columns[i][0][first + i : first + i + 1]
            pivots[own] = jnp.where(in_group == first + i, pivot, pivots[own])
            rows[i] = rows[i] / pivot
            for j in range(i + 1, PANEL):
                entry = columns[i][0][first + j : first + j + 1]
                rows[j] = rows[j] - entry * rows[i]
                factor = entry / pivot
                columns[j] = [old - factor * left for old, left in zip(columns[j], columns[i])]
            columns[i][0] = jnp.where(in_group > first + i, columns[i][0], 0.0)
        for g in range(own, len(groups)):
            for i in range(PANEL):
                groups[g] = groups[g] - columns[i][g - own] * rows[i]
    work = jnp.concatenate([group / jnp.sqrt(pivot) for group, pivot in zip(groups, pivots)], axis=0)
    inverse = jnp.where((at_lane >= SHIFT) & (at_lane < INNER), work, 0.0)
    columns = jnp.concatenate([product_ref[...], basis_ref[...].astype(jnp.float32)], axis=1)
    tall = jnp.concatenate(
        [jnp.zeros((SHIFT, 2 * PAIR), jnp.float32), columns, jnp.zeros((PAIR - INNER, 2 * PAIR), jnp.float32)], axis=0
    )
    both_ref[:, :K] = jnp.dot(inverse, tall, precision=HIGHEST).T
    flat = jnp.concatenate([both_ref[pl.ds(j, 32, stride=8), :][:, :K] for j in range(8)], axis=1)
    for j in range(8):
        lanes = slice(8 * K * j, 8 * K * (j + 1))
        out_c_ref[:, lanes] = jnp.concatenate([flat[j : j + 1], flat[8 + j : 9 + j]], axis=0).astype(jnp.bfloat16)
        out_u_ref[:, lanes] = jnp.concatenate([flat[16 + j : 17 + j], flat[24 + j : 25 + j]], axis=0).astype(jnp.bfloat16)
    inner = work[:, INNER : INNER + 1] * (1.0 / math.sqrt(TOTAL))
    coeff_ref[...] = jnp.sum(jnp.where(at_lane == at_row, inner, 0.0), axis=0)[:K]


def summed(array, axes, count):
    copies = jnp.broadcast_to(array[None], (count,) + array.shape)
    return jnp.sum(lax.all_to_all(copies, axes, 0, 0, tiled=True), axis=0)


def per_device(tangent, block_row, block_col, tile_count, old_basis, old_id, residual):
    params = pltpu.CompilerParams(vmem_limit_bytes=VMEM)
    smem = pl.BlockSpec(memory_space=pltpu.SMEM)
    vmem = pl.BlockSpec(memory_space=pltpu.VMEM)
    first, second = (old_basis[i].reshape(BLK, K).T for i in (0, 1))
    kept = old_id[0] % 2 == 0
    sideways = jnp.concatenate([jnp.where(kept, first, second), jnp.where(kept, second, first)], axis=1)
    placed = lax.ppermute(sideways, COL, [(i, (i + 1) % N_COL) for i in range(N_COL)])
    rows, cols = block_row.reshape(NNZ), block_col.reshape(NNZ)
    owner = rows >> 1
    side = jnp.where(jnp.arange(NNZ) < tile_count.reshape(1), rows & 1, 2)
    slots = (owner & (N_NEAR - 1)) * N_Z_HI + (owner >> 3) + (side << 6) + (cols << 8)
    at_row = lax.broadcasted_iota(jnp.int32, (PAIR - K, PAIR), 0)
    extra = jnp.where((at_row == 1) | (at_row == K), residual.reshape(1, PAIR), 0.0)
    blocks, slots, extra, sent = lax.optimization_barrier((tangent.reshape(NNZ, BLK, BLK), slots, extra, placed))
    copies = jnp.broadcast_to(sent[None], (N_ROW, K, PAIR))
    col_basis = lax.all_to_all(copies, ROW, 0, 0, tiled=True)
    partial = pl.pallas_call(
        product_kernel,
        out_shape=jax.ShapeDtypeStruct((N_COL, WORDS, PAIR), jnp.int32),
        in_specs=[smem, vmem, vmem],
        out_specs=vmem,
        scratch_shapes=[pltpu.VMEM((2 * N_ROW, K, BLK), jnp.bfloat16), pltpu.VMEM((N_COL, K, PAIR), jnp.float32)],
        compiler_params=params,
    )(slots, blocks, col_basis)
    near = lax.all_to_all(partial, NEAR, 0, 0, tiled=True)
    near = pl.pallas_call(
        near_kernel,
        out_shape=jax.ShapeDtypeStruct((N_Z_HI, WORDS, PAIR), jnp.int32),
        in_specs=[vmem],
        out_specs=vmem,
        scratch_shapes=[pltpu.VMEM((N_NEAR, K, PAIR), jnp.float32), pltpu.VMEM((N_Z_HI, K, PAIR), jnp.float32)],
        compiler_params=params,
    )(near.reshape(N_NEAR, N_Z_HI, WORDS, PAIR))
    far = lax.all_to_all(near, "z_hi", 0, 0, tiled=True)
    product, gram = pl.pallas_call(
        gram_kernel,
        out_shape=(
            jax.ShapeDtypeStruct((K, PAIR), jnp.float32),
            jax.ShapeDtypeStruct((HALF, PAIR), jnp.float32),
        ),
        in_specs=[vmem, vmem],
        out_specs=(vmem, vmem),
        compiler_params=params,
    )(far, extra)
    gram = summed(gram, ("core",) + NEAR, N_CORE * N_NEAR)
    gram = summed(gram, "y", N_Y)
    gram = summed(gram, "z_hi", N_Z_HI)
    out_c, out_u, coefficients = pl.pallas_call(
        finish_kernel,
        out_shape=(
            jax.ShapeDtypeStruct((2, BLK * K), jnp.bfloat16),
            jax.ShapeDtypeStruct((2, BLK * K), jnp.bfloat16),
            jax.ShapeDtypeStruct((K,), jnp.float32),
        ),
        in_specs=[vmem, vmem, vmem],
        out_specs=(vmem, vmem, vmem),
        scratch_shapes=[pltpu.VMEM((2 * PAIR, PAIR), jnp.float32)],
        compiler_params=params,
    )(gram, product, placed)
    return (out_c, out_u, coefficients)


def solution(mesh):
    split = Mesh(mesh.devices.reshape(N_Y, N_CORE, N_Z_HI, N_Z_LO, N_X), ROW + COL)
    return jax.shard_map(
        per_device,
        mesh=split,
        in_specs=(
            P(ROW, COL, None, None),
            P(ROW, COL, None),
            P(ROW, COL, None),
            P(ROW, COL),
            P(ROW + COL, None),
            P(ROW + COL),
            P(ROW + COL),
        ),
        out_specs=(P(ROW + COL, None), P(ROW + COL, None), P()),
        check_vma=False,
    )
```

```python
import math

import jax
import jax.numpy as jnp
from jax import lax
from jax.experimental import pallas as pl
from jax.experimental.pallas import tpu as pltpu
from jax.sharding import Mesh
from jax.sharding import PartitionSpec as P

BLK = 64
K = 48
PAIR = 2 * BLK
N_X, N_Y, N_CORE = 4, 8, 2
N_Z_HI, N_Z_LO = 8, 2
ROW = ("y", "core")
NEAR = ("z_lo", "x")
COL = ("z_hi",) + NEAR
N_ROW = N_Y * N_CORE
N_NEAR = N_Z_LO * N_X
N_COL = N_Z_HI * N_NEAR
NNZ = 64
TOTAL = N_ROW * N_COL * PAIR
HIGHEST = lax.Precision.HIGHEST
VMEM = 48 * 1024 * 1024


HALF = BLK // 4
PANEL = 8
BATCH = 64
SHIFT = K
INNER = 2 * K
WORDS = 2 * HALF
STEPS = (64, 32, 16, 8, 4, 2, 1)
LOWEST = 100
MAGIC = 12582912.0


def encode(sums_ref, count, out_ref):
    def look(i, peak):
        return jnp.maximum(peak, jnp.abs(sums_ref[i]))

    peak = lax.fori_loop(0, count, look, jnp.zeros((K, PAIR), jnp.float32), unroll=min(count, 16))
    peak = jnp.broadcast_to(jnp.max(peak, axis=1, keepdims=True), (K, PAIR))
    factor = jnp.full((K, PAIR), 2.0**19, jnp.float32)
    power = jnp.zeros((K, PAIR), jnp.int32)
    for step in STEPS:
        big = peak >= 2.0**step
        peak = jnp.where(big, peak * 2.0**-step, peak)
        factor = jnp.where(big, factor * 2.0**-step, factor)
        power = jnp.where(big, power + step, power)
    for step in STEPS:
        small = (peak < 2.0 ** (1 - step)) & (power - step >= -LOWEST)
        peak = jnp.where(small, peak * 2.0**step, peak)
        factor = jnp.where(small, factor * 2.0**step, factor)
        power = jnp.where(small, power - step, power)
    power = power + LOWEST
    lane = lax.broadcasted_iota(jnp.int32, (HALF, PAIR), 1)
    shown = jnp.where(lane < 8, power[:HALF], jnp.where(lane < 16, power[HALF:WORDS], power[WORDS:]))
    flags = ((shown >> (lane & 7)) & 1) << 10

    def put(i, carry):
        code = ((sums_ref[i] * factor + MAGIC) - MAGIC).astype(jnp.int32)
        code = jnp.minimum(code, (1 << 20) - 1)
        third = code[WORDS:]
        out_ref[i, :HALF] = (code[:HALF] << 11) | ((third >> 10) & 0x7FF)
        out_ref[i, HALF:] = (code[HALF:WORDS] << 11) | (third & 0x3FF) | flags
        return carry

    lax.fori_loop(0, count, put, 0, unroll=min(count, 16))


def unit_of(second):
    lane = lax.broadcasted_iota(jnp.int32, (HALF, PAIR), 1)
    bits = (((second >> 10) & 1) << (lane & 7)).astype(jnp.float32)
    power = jnp.concatenate(
        [
            jnp.sum(jnp.where((lane >= 8 * i) & (lane < 8 * i + 8), bits, 0.0), axis=1, keepdims=True)
            for i in range(3)
        ],
        axis=0,
    )
    power = jnp.broadcast_to(power, (K, PAIR)).astype(jnp.int32)
    unit = jnp.full((K, PAIR), 2.0 ** (-LOWEST - 19), jnp.float32)
    for i in range(8):
        steps = (2.0 ** (1 << i),) if i < 7 else (2.0**64, 2.0**64)
        for step in steps:
            unit = jnp.where(((power >> i) & 1) == 1, unit * step, unit)
    return unit


def decode(words):
    first, second = words[:HALF], words[HALF:]
    third = ((first << 21) >> 11) | (second & 0x3FF)
    return jnp.concatenate([first >> 11, second >> 11, third], axis=0).astype(jnp.float32)


def near_kernel(near_ref, out_ref, unit_ref, sums_ref):
    for source in range(N_NEAR):
        unit_ref[source] = unit_of(near_ref[source, 0, HALF:])

    for i in range(N_Z_HI):
        total = decode(near_ref[0, i]) * unit_ref[0]
        for source in range(1, N_NEAR):
            total += decode(near_ref[source, i]) * unit_ref[source]
        sums_ref[i] = total
    encode(sums_ref, N_Z_HI, out_ref)


def product_kernel(slot_ref, tangent_ref, basis_ref, out_ref, half_ref, sums_ref):
    for q in range(N_ROW):
        half_ref[2 * q] = basis_ref[q, :, :BLK]
        half_ref[2 * q + 1] = basis_ref[q, :, BLK:]
    sums_ref[...] = jnp.zeros_like(sums_ref)

    side_of_lane = lax.broadcasted_iota(jnp.int32, (K, PAIR), 1) >> 6

    def add_blocks(step, carry):
        places, products = [], []
        for i in range(BATCH):
            n = step * BATCH + i
            slot = slot_ref[n]
            places.append(slot & (N_COL - 1))
            side = (slot >> 6) & 3
            product = lax.dot_general(
                half_ref[slot >> 8], tangent_ref[n], (((1,), (1,)), ((), ())), preferred_element_type=jnp.float32
            )
            products.append(jnp.where(side_of_lane == side, jnp.concatenate([product, product], axis=1), 0.0))
        for place, product in zip(places, products):
            sums_ref[place] += product
        return carry

    lax.fori_loop(0, NNZ // BATCH, add_blocks, 0)
    encode(sums_ref, N_COL, out_ref)


def gram_kernel(far_ref, extra_ref, product_ref, gram_ref):
    product = decode(far_ref[0]) * unit_of(far_ref[0, HALF:])
    for source in range(1, N_Z_HI):
        product += decode(far_ref[source]) * unit_of(far_ref[source, HALF:])
    product_ref[...] = product
    both = jnp.concatenate([product, extra_ref[...]], axis=0)
    gram = lax.dot_general(product, both, (((1,), (1,)), ((), ())), precision=HIGHEST)
    lane = lax.broadcasted_iota(jnp.int32, (HALF, PAIR), 1)
    top, middle, bottom = gram[:HALF], gram[HALF:WORDS], gram[WORDS:]
    gram_ref[...] = jnp.where(
        (lane < K) | (lane == 96),
        bottom,
        jnp.where((lane < 80) | (lane == 97), pltpu.roll(middle, 48, 1), pltpu.roll(top, 112, 1)),
    )


def finish_kernel(gram_ref, product_ref, basis_ref, out_c_ref, out_u_ref, coeff_ref, both_ref):
    packed = gram_ref[...]
    top = pltpu.roll(packed, 16, 1)
    blocks = jnp.concatenate([top, pltpu.roll(packed, 80, 1), packed], axis=0)
    inner = jnp.concatenate([top, pltpu.roll(packed, 127, 1), packed], axis=0)
    at_row = lax.broadcasted_iota(jnp.int32, (K, PAIR), 0)
    at_lane = lax.broadcasted_iota(jnp.int32, (K, PAIR), 1)
    blocks = blocks * (1.0 / TOTAL)
    below = jnp.concatenate([jnp.where(at_lane < at_row, blocks, 0.0), jnp.zeros((PAIR - K, PAIR), jnp.float32)], axis=0)
    work = jnp.where(at_lane <= at_row, blocks, below.T[:K])
    work = jnp.where(at_lane == INNER, inner, work)
    work = jnp.where(at_lane == at_row + SHIFT, 1.0, work)
    groups = [work[i : i + 8] for i in range(0, K, 8)]
    in_group = at_row[:8]
    pivots = [jnp.ones((8, PAIR), jnp.float32)] * len(groups)
    for start in range(0, K, PANEL):
        own = start // 8
        first = start % 8
        columns = [
            [jnp.broadcast_to(group[:, k : k + 1], (8, PAIR)) for group in groups[own:]]
            for k in range(start, start + PANEL)
        ]
        rows = [groups[own][first + i : first + i + 1] for i in range(PANEL)]
        for i in range(PANEL):
            pivot = columns[i][0][first + i : first + i + 1]
            pivots[own] = jnp.where(in_group == first + i, pivot, pivots[own])
            rows[i] = rows[i] / pivot
            for j in range(i + 1, PANEL):
                entry = columns[i][0][first + j : first + j + 1]
                rows[j] = rows[j] - entry * rows[i]
                factor = entry / pivot
                columns[j] = [old - factor * left for old, left in zip(columns[j], columns[i])]
            columns[i][0] = jnp.where(in_group > first + i, columns[i][0], 0.0)
        for g in range(own, len(groups)):
            for i in range(PANEL):
                groups[g] = groups[g] - columns[i][g - own] * rows[i]
    work = jnp.concatenate([group / jnp.sqrt(pivot) for group, pivot in zip(groups, pivots)], axis=0)
    inverse = jnp.where((at_lane >= SHIFT) & (at_lane < INNER), work, 0.0)
    columns = jnp.concatenate([product_ref[...], basis_ref[...].astype(jnp.float32)], axis=1)
    tall = jnp.concatenate(
        [jnp.zeros((SHIFT, 2 * PAIR), jnp.float32), columns, jnp.zeros((PAIR - INNER, 2 * PAIR), jnp.float32)], axis=0
    )
    both_ref[:, :K] = jnp.dot(inverse, tall, precision=HIGHEST).T
    flat = jnp.concatenate([both_ref[pl.ds(j, 32, stride=8), :][:, :K] for j in range(8)], axis=1)
    for j in range(8):
        lanes = slice(8 * K * j, 8 * K * (j + 1))
        out_c_ref[:, lanes] = jnp.concatenate([flat[j : j + 1], flat[8 + j : 9 + j]], axis=0).astype(jnp.bfloat16)
        out_u_ref[:, lanes] = jnp.concatenate([flat[16 + j : 17 + j], flat[24 + j : 25 + j]], axis=0).astype(jnp.bfloat16)
    inner = work[:, INNER : INNER + 1] * (1.0 / math.sqrt(TOTAL))
    coeff_ref[...] = jnp.sum(jnp.where(at_lane == at_row, inner, 0.0), axis=0)[:K]


def summed(array, axes, count):
    copies = jnp.broadcast_to(array[None], (count,) + array.shape)
    return jnp.sum(lax.all_to_all(copies, axes, 0, 0, tiled=True), axis=0)


def per_device(tangent, block_row, block_col, tile_count, old_basis, old_id, residual):
    params = pltpu.CompilerParams(vmem_limit_bytes=VMEM)
    smem = pl.BlockSpec(memory_space=pltpu.SMEM)
    vmem = pl.BlockSpec(memory_space=pltpu.VMEM)
    first, second = (old_basis[i].reshape(BLK, K).T for i in (0, 1))
    kept = old_id[0] % 2 == 0
    sideways = jnp.concatenate([jnp.where(kept, first, second), jnp.where(kept, second, first)], axis=1)
    placed = lax.ppermute(sideways, COL, [(i, (i + 1) % N_COL) for i in range(N_COL)])
    rows, cols = block_row.reshape(NNZ), block_col.reshape(NNZ)
    owner = rows >> 1
    side = jnp.where(jnp.arange(NNZ) < tile_count.reshape(1), rows & 1, 2)
    slots = (owner & (N_NEAR - 1)) * N_Z_HI + (owner >> 3) + (side << 6) + (cols << 8)
    at_row = lax.broadcasted_iota(jnp.int32, (PAIR - K, PAIR), 0)
    extra = jnp.where((at_row == 1) | (at_row == K), residual.reshape(1, PAIR), 0.0)
    blocks, slots, extra, sent = lax.optimization_barrier((tangent.reshape(NNZ, BLK, BLK), slots, extra, placed))
    copies = jnp.broadcast_to(sent[None], (N_ROW, K, PAIR))
    col_basis = lax.all_to_all(copies, ROW, 0, 0, tiled=True)
    partial = pl.pallas_call(
        product_kernel,
        out_shape=jax.ShapeDtypeStruct((N_COL, WORDS, PAIR), jnp.int32),
        in_specs=[smem, vmem, vmem],
        out_specs=vmem,
        scratch_shapes=[pltpu.VMEM((2 * N_ROW, K, BLK), jnp.bfloat16), pltpu.VMEM((N_COL, K, PAIR), jnp.float32)],
        compiler_params=params,
    )(slots, blocks, col_basis)
    near = lax.all_to_all(partial, NEAR, 0, 0, tiled=True)
    near = pl.pallas_call(
        near_kernel,
        out_shape=jax.ShapeDtypeStruct((N_Z_HI, WORDS, PAIR), jnp.int32),
        in_specs=[vmem],
        out_specs=vmem,
        scratch_shapes=[pltpu.VMEM((N_NEAR, K, PAIR), jnp.float32), pltpu.VMEM((N_Z_HI, K, PAIR), jnp.float32)],
        compiler_params=params,
    )(near.reshape(N_NEAR, N_Z_HI, WORDS, PAIR))
    far = lax.all_to_all(near, "z_hi", 0, 0, tiled=True)
    product, gram = pl.pallas_call(
        gram_kernel,
        out_shape=(
            jax.ShapeDtypeStruct((K, PAIR), jnp.float32),
            jax.ShapeDtypeStruct((HALF, PAIR), jnp.float32),
        ),
        in_specs=[vmem, vmem],
        out_specs=(vmem, vmem),
        compiler_params=params,
    )(far, extra)
    gram = summed(gram, ("core",) + NEAR, N_CORE * N_NEAR)
    gram = summed(gram, "y", N_Y)
    gram = summed(gram, "z_hi", N_Z_HI)
    out_c, out_u, coefficients = pl.pallas_call(
        finish_kernel,
        out_shape=(
            jax.ShapeDtypeStruct((2, BLK * K), jnp.bfloat16),
            jax.ShapeDtypeStruct((2, BLK * K), jnp.bfloat16),
            jax.ShapeDtypeStruct((K,), jnp.float32),
        ),
        in_specs=[vmem, vmem, vmem],
        out_specs=(vmem, vmem, vmem),
        scratch_shapes=[pltpu.VMEM((2 * PAIR, PAIR), jnp.float32)],
        compiler_params=params,
    )(gram, product, placed)
    return (out_c, out_u, coefficients)


def solution(mesh):
    split = Mesh(mesh.devices.reshape(N_Y, N_CORE, N_Z_HI, N_Z_LO, N_X), ROW + COL)
    return jax.shard_map(
        per_device,
        mesh=split,
        in_specs=(
            P(ROW, COL, None, None),
            P(ROW, COL, None),
            P(ROW, COL, None),
            P(ROW, COL),
            P(ROW + COL, None),
            P(ROW + COL),
            P(ROW + COL),
        ),
        out_specs=(P(ROW + COL, None), P(ROW + COL, None), P()),
        check_vma=False,
    )
```

```python
import math

import jax
import jax.numpy as jnp
from jax import lax
from jax.experimental import pallas as pl
from jax.experimental.pallas import tpu as pltpu
from jax.sharding import Mesh
from jax.sharding import PartitionSpec as P

BLK = 64
K = 48
PAIR = 2 * BLK
N_X, N_Y, N_CORE = 4, 8, 2
N_Z_HI, N_Z_LO = 8, 2
ROW = ("y", "core")
NEAR = ("z_lo", "x")
COL = ("z_hi",) + NEAR
N_ROW = N_Y * N_CORE
N_NEAR = N_Z_LO * N_X
N_COL = N_Z_HI * N_NEAR
NNZ = 64
TOTAL = N_ROW * N_COL * PAIR
HIGHEST = lax.Precision.HIGHEST
VMEM = 48 * 1024 * 1024


HALF = BLK // 4
PANEL = 8
BATCH = 64
SHIFT = K
INNER = 2 * K
WORDS = 2 * HALF
STEPS = (64, 32, 16, 8, 4, 2, 1)
LOWEST = 100
MAGIC = 12582912.0


def encode(sums_ref, count, out_ref):
    def look(i, peak):
        return jnp.maximum(peak, jnp.abs(sums_ref[i]))

    peak = lax.fori_loop(0, count, look, jnp.zeros((K, PAIR), jnp.float32), unroll=min(count, 16))
    peak = jnp.broadcast_to(jnp.max(peak, axis=1, keepdims=True), (K, PAIR))
    factor = jnp.full((K, PAIR), 2.0**19, jnp.float32)
    power = jnp.zeros((K, PAIR), jnp.int32)
    for step in STEPS:
        big = peak >= 2.0**step
        peak = jnp.where(big, peak * 2.0**-step, peak)
        factor = jnp.where(big, factor * 2.0**-step, factor)
        power = jnp.where(big, power + step, power)
    for step in STEPS:
        small = (peak < 2.0 ** (1 - step)) & (power - step >= -LOWEST)
        peak = jnp.where(small, peak * 2.0**step, peak)
        factor = jnp.where(small, factor * 2.0**step, factor)
        power = jnp.where(small, power - step, power)
    power = power + LOWEST
    lane = lax.broadcasted_iota(jnp.int32, (HALF, PAIR), 1)
    shown = jnp.where(lane < 8, power[:HALF], jnp.where(lane < 16, power[HALF:WORDS], power[WORDS:]))
    flags = ((shown >> (lane & 7)) & 1) << 10

    def put(i, carry):
        code = ((sums_ref[i] * factor + MAGIC) - MAGIC).astype(jnp.int32)
        code = jnp.minimum(code, (1 << 20) - 1)
        third = code[WORDS:]
        out_ref[i, :HALF] = (code[:HALF] << 11) | ((third >> 10) & 0x7FF)
        out_ref[i, HALF:] = (code[HALF:WORDS] << 11) | (third & 0x3FF) | flags
        return carry

    lax.fori_loop(0, count, put, 0, unroll=min(count, 16))


def unit_of(second):
    lane = lax.broadcasted_iota(jnp.int32, (HALF, PAIR), 1)
    bits = (((second >> 10) & 1) << (lane & 7)).astype(jnp.float32)
    power = jnp.concatenate(
        [
            jnp.sum(jnp.where((lane >= 8 * i) & (lane < 8 * i + 8), bits, 0.0), axis=1, keepdims=True)
            for i in range(3)
        ],
        axis=0,
    )
    power = jnp.broadcast_to(power, (K, PAIR)).astype(jnp.int32)
    unit = jnp.full((K, PAIR), 2.0 ** (-LOWEST - 19), jnp.float32)
    for i in range(8):
        steps = (2.0 ** (1 << i),) if i < 7 else (2.0**64, 2.0**64)
        for step in steps:
            unit = jnp.where(((power >> i) & 1) == 1, unit * step, unit)
    return unit


def decode(words):
    first, second = words[:HALF], words[HALF:]
    third = ((first << 21) >> 11) | (second & 0x3FF)
    return jnp.concatenate([first >> 11, second >> 11, third], axis=0).astype(jnp.float32)


def near_kernel(near_ref, out_ref, unit_ref, sums_ref):
    for source in range(N_NEAR):
        unit_ref[source] = unit_of(near_ref[source, 0, HALF:])

    for i in range(N_Z_HI):
        total = decode(near_ref[0, i]) * unit_ref[0]
        for source in range(1, N_NEAR):
            total += decode(near_ref[source, i]) * unit_ref[source]
        sums_ref[i] = total
    encode(sums_ref, N_Z_HI, out_ref)


def product_kernel(slot_ref, tangent_ref, basis_ref, out_ref, half_ref, sums_ref):
    for q in range(N_ROW):
        half_ref[2 * q] = basis_ref[q, :, :BLK]
        half_ref[2 * q + 1] = basis_ref[q, :, BLK:]
    sums_ref[...] = jnp.zeros_like(sums_ref)

    side_of_lane = lax.broadcasted_iota(jnp.int32, (K, PAIR), 1) >> 6

    def add_blocks(step, carry):
        places, products = [], []
        for i in range(BATCH):
            n = step * BATCH + i
            slot = slot_ref[n]
            places.append(slot & (N_COL - 1))
            side = (slot >> 6) & 3
            product = lax.dot_general(
                half_ref[slot >> 8], tangent_ref[n], (((1,), (1,)), ((), ())), preferred_element_type=jnp.float32
            )
            products.append(jnp.where(side_of_lane == side, jnp.concatenate([product, product], axis=1), 0.0))
        for place, product in zip(places, products):
            sums_ref[place] += product
        return carry

    lax.fori_loop(0, NNZ // BATCH, add_blocks, 0)
    encode(sums_ref, N_COL, out_ref)


def gram_kernel(far_ref, extra_ref, product_ref, gram_ref):
    product = decode(far_ref[0]) * unit_of(far_ref[0, HALF:])
    for source in range(1, N_Z_HI):
        product += decode(far_ref[source]) * unit_of(far_ref[source, HALF:])
    product_ref[...] = product
    both = jnp.concatenate([product, extra_ref[...]], axis=0)
    gram = lax.dot_general(product, both, (((1,), (1,)), ((), ())), precision=HIGHEST)
    row = lax.broadcasted_iota(jnp.int32, (HALF, PAIR), 0)
    lane = lax.broadcasted_iota(jnp.int32, (HALF, PAIR), 1)

    def by_lane(bottom, middle, top):
        return jnp.where(lane < K, bottom, jnp.where(lane < 80, middle, top))

    top, middle, bottom = gram[:HALF], gram[HALF:WORDS], gram[WORDS:]
    packed = by_lane(bottom, pltpu.roll(middle, K, 1), pltpu.roll(top, 80, 1))
    inner = by_lane(*(jnp.broadcast_to(part[:, INNER : INNER + 1], (HALF, PAIR)) for part in (bottom, middle, top)))
    place = lane - by_lane(32, 64, 80)
    packed = jnp.where(place == row + 1, inner, packed)
    packed = jnp.where((place == 2) & (row == 0), inner[HALF - 1 :], packed)
    gram_ref[...] = jnp.concatenate([packed[i : i + 4, : 2 * K] for i in range(0, HALF, 4)], axis=1)


def finish_kernel(gram_ref, product_ref, basis_ref, out_c_ref, out_u_ref, coeff_ref, both_ref):
    wide = gram_ref[...]
    packed = jnp.concatenate([wide[:, 2 * K * i : 2 * K * (i + 1)] for i in range(4)], axis=0)
    packed = jnp.concatenate([packed, jnp.zeros((HALF, PAIR - 2 * K), jnp.float32)], axis=1)
    blocks = jnp.concatenate([pltpu.roll(packed, K, 1), pltpu.roll(packed, 80, 1), packed], axis=0)
    at_row = lax.broadcasted_iota(jnp.int32, (K, PAIR), 0)
    at_lane = lax.broadcasted_iota(jnp.int32, (K, PAIR), 1)
    inner = jnp.sum(jnp.where(at_lane == at_row + 1, blocks, 0.0), axis=1, keepdims=True)
    last = jnp.sum(jnp.where(at_lane == at_row + 2, blocks, 0.0), axis=1, keepdims=True)
    last = jnp.concatenate([jnp.broadcast_to(last[i : i + 1], (HALF, 1)) for i in range(0, K, HALF)], axis=0)
    inner = jnp.where((at_row & (HALF - 1)) == HALF - 1, last, inner)
    blocks = blocks * (1.0 / TOTAL)
    below = jnp.concatenate([jnp.where(at_lane < at_row, blocks, 0.0), jnp.zeros((PAIR - K, PAIR), jnp.float32)], axis=0)
    work = jnp.where(at_lane <= at_row, blocks, below.T[:K])
    work = jnp.where(at_lane == INNER, inner, work)
    work = jnp.where(at_lane == at_row + SHIFT, 1.0, work)
    groups = [work[i : i + 8] for i in range(0, K, 8)]
    in_group = at_row[:8]
    pivots = [jnp.ones((8, PAIR), jnp.float32)] * len(groups)
    for start in range(0, K, PANEL):
        own = start // 8
        first = start % 8
        columns = [
            [jnp.broadcast_to(group[:, k : k + 1], (8, PAIR)) for group in groups[own:]]
            for k in range(start, start + PANEL)
        ]
        rows = [groups[own][first + i : first + i + 1] for i in range(PANEL)]
        for i in range(PANEL):
            pivot = columns[i][0][first + i : first + i + 1]
            pivots[own] = jnp.where(in_group == first + i, pivot, pivots[own])
            inverse = 1.0 / pivot
            rows[i] = rows[i] * inverse
            for j in range(i + 1, PANEL):
                entry = columns[i][0][first + j : first + j + 1]
                rows[j] = rows[j] - entry * rows[i]
                factor = entry * inverse
                columns[j] = [old - factor * left for old, left in zip(columns[j], columns[i])]
            columns[i][0] = jnp.where(in_group > first + i, columns[i][0], 0.0)
        for g in range(own, len(groups)):
            for i in range(PANEL):
                groups[g] = groups[g] - columns[i][g - own] * rows[i]
    work = jnp.concatenate([group / jnp.sqrt(pivot) for group, pivot in zip(groups, pivots)], axis=0)
    inverse = jnp.where((at_lane >= SHIFT) & (at_lane < INNER), work, 0.0)
    columns = jnp.concatenate([product_ref[...], basis_ref[...].astype(jnp.float32)], axis=1)
    tall = jnp.concatenate(
        [jnp.zeros((SHIFT, 2 * PAIR), jnp.float32), columns, jnp.zeros((PAIR - INNER, 2 * PAIR), jnp.float32)], axis=0
    )
    both_ref[:, :K] = jnp.dot(inverse, tall, precision=HIGHEST).T
    flat = jnp.concatenate([both_ref[pl.ds(j, 32, stride=8), :][:, :K] for j in range(8)], axis=1)
    for j in range(8):
        lanes = slice(8 * K * j, 8 * K * (j + 1))
        out_c_ref[:, lanes] = jnp.concatenate([flat[j : j + 1], flat[8 + j : 9 + j]], axis=0).astype(jnp.bfloat16)
        out_u_ref[:, lanes] = jnp.concatenate([flat[16 + j : 17 + j], flat[24 + j : 25 + j]], axis=0).astype(jnp.bfloat16)
    inner = work[:, INNER : INNER + 1] * (1.0 / math.sqrt(TOTAL))
    coeff_ref[...] = jnp.sum(jnp.where(at_lane == at_row, inner, 0.0), axis=0)[:K]


def summed(array, axes, count):
    copies = jnp.broadcast_to(array[None], (count,) + array.shape)
    return jnp.sum(lax.all_to_all(copies, axes, 0, 0, tiled=True), axis=0)


def per_device(tangent, block_row, block_col, tile_count, old_basis, old_id, residual):
    params = pltpu.CompilerParams(vmem_limit_bytes=VMEM)
    smem = pl.BlockSpec(memory_space=pltpu.SMEM)
    vmem = pl.BlockSpec(memory_space=pltpu.VMEM)
    first, second = (old_basis[i].reshape(BLK, K).T for i in (0, 1))
    kept = old_id[0] % 2 == 0
    sideways = jnp.concatenate([jnp.where(kept, first, second), jnp.where(kept, second, first)], axis=1)
    placed = lax.ppermute(sideways, COL, [(i, (i + 1) % N_COL) for i in range(N_COL)])
    rows, cols = block_row.reshape(NNZ), block_col.reshape(NNZ)
    owner = rows >> 1
    side = jnp.where(jnp.arange(NNZ) < tile_count.reshape(1), rows & 1, 2)
    slots = (owner & (N_NEAR - 1)) * N_Z_HI + (owner >> 3) + (side << 6) + (cols << 8)
    at_row = lax.broadcasted_iota(jnp.int32, (PAIR - K, PAIR), 0)
    extra = jnp.where(at_row == K, residual.reshape(1, PAIR), 0.0)
    blocks, slots, extra, sent = lax.optimization_barrier((tangent.reshape(NNZ, BLK, BLK), slots, extra, placed))
    copies = jnp.broadcast_to(sent[None], (N_ROW, K, PAIR))
    col_basis = lax.all_to_all(copies, ROW, 0, 0, tiled=True)
    partial = pl.pallas_call(
        product_kernel,
        out_shape=jax.ShapeDtypeStruct((N_COL, WORDS, PAIR), jnp.int32),
        in_specs=[smem, vmem, vmem],
        out_specs=vmem,
        scratch_shapes=[pltpu.VMEM((2 * N_ROW, K, BLK), jnp.bfloat16), pltpu.VMEM((N_COL, K, PAIR), jnp.float32)],
        compiler_params=params,
    )(slots, blocks, col_basis)
    near = lax.all_to_all(partial, NEAR, 0, 0, tiled=True)
    near = pl.pallas_call(
        near_kernel,
        out_shape=jax.ShapeDtypeStruct((N_Z_HI, WORDS, PAIR), jnp.int32),
        in_specs=[vmem],
        out_specs=vmem,
        scratch_shapes=[pltpu.VMEM((N_NEAR, K, PAIR), jnp.float32), pltpu.VMEM((N_Z_HI, K, PAIR), jnp.float32)],
        compiler_params=params,
    )(near.reshape(N_NEAR, N_Z_HI, WORDS, PAIR))
    far = lax.all_to_all(near, "z_hi", 0, 0, tiled=True)
    product, gram = pl.pallas_call(
        gram_kernel,
        out_shape=(
            jax.ShapeDtypeStruct((K, PAIR), jnp.float32),
            jax.ShapeDtypeStruct((4, 4 * 2 * K), jnp.float32),
        ),
        in_specs=[vmem, vmem],
        out_specs=(vmem, vmem),
        compiler_params=params,
    )(far, extra)
    gram = summed(gram, ("core",) + NEAR, N_CORE * N_NEAR)
    gram = summed(gram, "z_hi", N_Z_HI)
    gram = summed(gram, "y", N_Y)
    out_c, out_u, coefficients = pl.pallas_call(
        finish_kernel,
        out_shape=(
            jax.ShapeDtypeStruct((2, BLK * K), jnp.bfloat16),
            jax.ShapeDtypeStruct((2, BLK * K), jnp.bfloat16),
            jax.ShapeDtypeStruct((K,), jnp.float32),
        ),
        in_specs=[vmem, vmem, vmem],
        out_specs=(vmem, vmem, vmem),
        scratch_shapes=[pltpu.VMEM((2 * PAIR, PAIR), jnp.float32)],
        compiler_params=params,
    )(gram, product, placed)
    return (out_c, out_u, coefficients)


def solution(mesh):
    split = Mesh(mesh.devices.reshape(N_Y, N_CORE, N_Z_HI, N_Z_LO, N_X), ROW + COL)
    return jax.shard_map(
        per_device,
        mesh=split,
        in_specs=(
            P(ROW, COL, None, None),
            P(ROW, COL, None),
            P(ROW, COL, None),
            P(ROW, COL),
            P(ROW + COL, None),
            P(ROW + COL),
            P(ROW + COL),
        ),
        out_specs=(P(ROW + COL, None), P(ROW + COL, None), P()),
        check_vma=False,
    )
```

```python
import math

import jax
import jax.numpy as jnp
from jax import lax
from jax.experimental import pallas as pl
from jax.experimental.pallas import tpu as pltpu
from jax.sharding import Mesh
from jax.sharding import PartitionSpec as P

BLK = 64
K = 48
PAIR = 2 * BLK
N_X, N_Y, N_CORE = 4, 8, 2
N_Z_HI, N_Z_LO = 8, 2
ROW = ("y", "core")
NEAR = ("z_lo", "x")
COL = ("z_hi",) + NEAR
N_ROW = N_Y * N_CORE
N_NEAR = N_Z_LO * N_X
N_COL = N_Z_HI * N_NEAR
NNZ = 64
TOTAL = N_ROW * N_COL * PAIR
HIGHEST = lax.Precision.HIGHEST
VMEM = 48 * 1024 * 1024


HALF = BLK // 4
PANEL = 8
BATCH = 64
SHIFT = K
INNER = 2 * K
WORDS = 2 * HALF
STEPS = (64, 32, 16, 8, 4, 2, 1)
LOWEST = 100
MAGIC = 12582912.0


def encode(sums_ref, count, out_ref):
    def look(i, peak):
        return jnp.maximum(peak, jnp.abs(sums_ref[i]))

    peak = lax.fori_loop(0, count, look, jnp.zeros((K, PAIR), jnp.float32), unroll=count)
    peak = jnp.broadcast_to(jnp.max(peak, axis=1, keepdims=True), (K, PAIR))
    factor = jnp.full((K, PAIR), 2.0**19, jnp.float32)
    power = jnp.zeros((K, PAIR), jnp.int32)
    for step in STEPS:
        big = peak >= 2.0**step
        peak = jnp.where(big, peak * 2.0**-step, peak)
        factor = jnp.where(big, factor * 2.0**-step, factor)
        power = jnp.where(big, power + step, power)
    for step in STEPS:
        small = (peak < 2.0 ** (1 - step)) & (power - step >= -LOWEST)
        peak = jnp.where(small, peak * 2.0**step, peak)
        factor = jnp.where(small, factor * 2.0**step, factor)
        power = jnp.where(small, power - step, power)
    power = power + LOWEST
    lane = lax.broadcasted_iota(jnp.int32, (HALF, PAIR), 1)
    shown = jnp.where(lane < 8, power[:HALF], jnp.where(lane < 16, power[HALF:WORDS], power[WORDS:]))
    flags = ((shown >> (lane & 7)) & 1) << 10

    def put(i, carry):
        code = ((sums_ref[i] * factor + MAGIC) - MAGIC).astype(jnp.int32)
        code = jnp.minimum(code, (1 << 20) - 1)
        third = code[WORDS:]
        out_ref[i, :HALF] = (code[:HALF] << 11) | ((third >> 10) & 0x7FF)
        out_ref[i, HALF:] = (code[HALF:WORDS] << 11) | (third & 0x3FF) | flags
        return carry

    lax.fori_loop(0, count, put, 0, unroll=count)


def unit_of(second):
    lane = lax.broadcasted_iota(jnp.int32, (HALF, PAIR), 1)
    bits = (((second >> 10) & 1) << (lane & 7)).astype(jnp.float32)
    power = jnp.concatenate(
        [
            jnp.sum(jnp.where((lane >= 8 * i) & (lane < 8 * i + 8), bits, 0.0), axis=1, keepdims=True)
            for i in range(3)
        ],
        axis=0,
    )
    power = jnp.broadcast_to(power, (K, PAIR)).astype(jnp.int32)
    unit = jnp.full((K, PAIR), 2.0 ** (-LOWEST - 19), jnp.float32)
    for i in range(8):
        steps = (2.0 ** (1 << i),) if i < 7 else (2.0**64, 2.0**64)
        for step in steps:
            unit = jnp.where(((power >> i) & 1) == 1, unit * step, unit)
    return unit


def decode(words):
    first, second = words[:HALF], words[HALF:]
    third = ((first << 21) >> 11) | (second & 0x3FF)
    return jnp.concatenate([first >> 11, second >> 11, third], axis=0).astype(jnp.float32)


def near_kernel(near_ref, out_ref, unit_ref, sums_ref):
    for source in range(N_NEAR):
        unit_ref[source] = unit_of(near_ref[source, 0, HALF:])

    for i in range(N_Z_HI):
        total = decode(near_ref[0, i]) * unit_ref[0]
        for source in range(1, N_NEAR):
            total += decode(near_ref[source, i]) * unit_ref[source]
        sums_ref[i] = total
    encode(sums_ref, N_Z_HI, out_ref)


def product_kernel(slot_ref, tangent_ref, basis_ref, out_ref, half_ref, sums_ref):
    for q in range(N_ROW):
        half_ref[2 * q] = basis_ref[q, :, :BLK]
        half_ref[2 * q + 1] = basis_ref[q, :, BLK:]
    sums_ref[...] = jnp.zeros_like(sums_ref)

    side_of_lane = lax.broadcasted_iota(jnp.int32, (K, PAIR), 1) >> 6

    def add_blocks(step, carry):
        places, products = [], []
        for i in range(BATCH):
            n = step * BATCH + i
            slot = slot_ref[n]
            places.append(slot & (N_COL - 1))
            side = (slot >> 6) & 3
            product = lax.dot_general(
                half_ref[slot >> 8], tangent_ref[n], (((1,), (1,)), ((), ())), preferred_element_type=jnp.float32
            )
            products.append(jnp.where(side_of_lane == side, jnp.concatenate([product, product], axis=1), 0.0))
        for place, product in zip(places, products):
            sums_ref[place] += product
        return carry

    lax.fori_loop(0, NNZ // BATCH, add_blocks, 0)
    encode(sums_ref, N_COL, out_ref)


def gram_kernel(far_ref, extra_ref, product_ref, gram_ref):
    product = decode(far_ref[0]) * unit_of(far_ref[0, HALF:])
    for source in range(1, N_Z_HI):
        product += decode(far_ref[source]) * unit_of(far_ref[source, HALF:])
    product_ref[...] = product
    both = jnp.concatenate([product, extra_ref[...]], axis=0)
    gram = lax.dot_general(product, both, (((1,), (1,)), ((), ())), precision=HIGHEST)
    row = lax.broadcasted_iota(jnp.int32, (HALF, PAIR), 0)
    lane = lax.broadcasted_iota(jnp.int32, (HALF, PAIR), 1)

    def by_lane(bottom, middle, top):
        return jnp.where(lane < K, bottom, jnp.where(lane < 80, middle, top))

    top, middle, bottom = gram[:HALF], gram[HALF:WORDS], gram[WORDS:]
    packed = by_lane(bottom, pltpu.roll(middle, K, 1), pltpu.roll(top, 80, 1))
    inner = by_lane(*(jnp.broadcast_to(part[:, INNER : INNER + 1], (HALF, PAIR)) for part in (bottom, middle, top)))
    place = lane - by_lane(32, 64, 80)
    packed = jnp.where(place == row + 1, inner, packed)
    packed = jnp.where((place == 2) & (row == 0), inner[HALF - 1 :], packed)
    gram_ref[...] = jnp.concatenate([packed[i : i + 4, : 2 * K] for i in range(0, HALF, 4)], axis=1)


def finish_kernel(gram_ref, product_ref, basis_ref, out_c_ref, out_u_ref, coeff_ref, both_ref):
    wide = gram_ref[...]
    packed = jnp.concatenate([wide[:, 2 * K * i : 2 * K * (i + 1)] for i in range(4)], axis=0)
    packed = jnp.concatenate([packed, jnp.zeros((HALF, PAIR - 2 * K), jnp.float32)], axis=1)
    blocks = jnp.concatenate([pltpu.roll(packed, K, 1), pltpu.roll(packed, 80, 1), packed], axis=0)
    at_row = lax.broadcasted_iota(jnp.int32, (K, PAIR), 0)
    at_lane = lax.broadcasted_iota(jnp.int32, (K, PAIR), 1)
    inner = jnp.sum(jnp.where(at_lane == at_row + 1, blocks, 0.0), axis=1, keepdims=True)
    last = jnp.sum(jnp.where(at_lane == at_row + 2, blocks, 0.0), axis=1, keepdims=True)
    last = jnp.concatenate([jnp.broadcast_to(last[i : i + 1], (HALF, 1)) for i in range(0, K, HALF)], axis=0)
    inner = jnp.where((at_row & (HALF - 1)) == HALF - 1, last, inner)
    blocks = blocks * (1.0 / TOTAL)
    below = jnp.concatenate([jnp.where(at_lane < at_row, blocks, 0.0), jnp.zeros((PAIR - K, PAIR), jnp.float32)], axis=0)
    work = jnp.where(at_lane <= at_row, blocks, below.T[:K])
    work = jnp.where(at_lane == INNER, inner, work)
    work = jnp.where(at_lane == at_row + SHIFT, 1.0, work)
    groups = [work[i : i + 8] for i in range(0, K, 8)]
    in_group = at_row[:8]
    pivots = [jnp.ones((8, PAIR), jnp.float32)] * len(groups)
    for start in range(0, K, PANEL):
        own = start // 8
        first = start % 8
        columns = [
            [jnp.broadcast_to(group[:, k : k + 1], (8, PAIR)) for group in groups[own:]]
            for k in range(start, start + PANEL)
        ]
        rows = [groups[own][first + i : first + i + 1] for i in range(PANEL)]
        for i in range(PANEL):
            pivot = columns[i][0][first + i : first + i + 1]
            pivots[own] = jnp.where(in_group == first + i, pivot, pivots[own])
            inverse = 1.0 / pivot
            rows[i] = rows[i] * inverse
            for j in range(i + 1, PANEL):
                entry = columns[i][0][first + j : first + j + 1]
                rows[j] = rows[j] - entry * rows[i]
                factor = entry * inverse
                columns[j] = [old - factor * left for old, left in zip(columns[j], columns[i])]
            columns[i][0] = jnp.where(in_group > first + i, columns[i][0], 0.0)
        for g in range(own, len(groups)):
            for i in range(PANEL):
                groups[g] = groups[g] - columns[i][g - own] * rows[i]
    work = jnp.concatenate([group / jnp.sqrt(pivot) for group, pivot in zip(groups, pivots)], axis=0)
    inverse = jnp.where((at_lane >= SHIFT) & (at_lane < INNER), work, 0.0)
    columns = jnp.concatenate([product_ref[...], basis_ref[...].astype(jnp.float32)], axis=1)
    tall = jnp.concatenate(
        [jnp.zeros((SHIFT, 2 * PAIR), jnp.float32), columns, jnp.zeros((PAIR - INNER, 2 * PAIR), jnp.float32)], axis=0
    )
    both_ref[:, :K] = jnp.dot(inverse, tall, precision=HIGHEST).T
    flat = jnp.concatenate([both_ref[pl.ds(j, 32, stride=8), :][:, :K] for j in range(8)], axis=1)
    for j in range(8):
        lanes = slice(8 * K * j, 8 * K * (j + 1))
        out_c_ref[:, lanes] = jnp.concatenate([flat[j : j + 1], flat[8 + j : 9 + j]], axis=0).astype(jnp.bfloat16)
        out_u_ref[:, lanes] = jnp.concatenate([flat[16 + j : 17 + j], flat[24 + j : 25 + j]], axis=0).astype(jnp.bfloat16)
    inner = work[:, INNER : INNER + 1] * (1.0 / math.sqrt(TOTAL))
    coeff_ref[...] = jnp.sum(jnp.where(at_lane == at_row, inner, 0.0), axis=0)[:K]


def summed(array, axes, count):
    copies = jnp.broadcast_to(array[None], (count,) + array.shape)
    return jnp.sum(lax.all_to_all(copies, axes, 0, 0, tiled=True), axis=0)


def per_device(tangent, block_row, block_col, tile_count, old_basis, old_id, residual):
    params = pltpu.CompilerParams(vmem_limit_bytes=VMEM)
    smem = pl.BlockSpec(memory_space=pltpu.SMEM)
    vmem = pl.BlockSpec(memory_space=pltpu.VMEM)
    first, second = (old_basis[i].reshape(BLK, K).T for i in (0, 1))
    kept = old_id[0] % 2 == 0
    sideways = jnp.concatenate([jnp.where(kept, first, second), jnp.where(kept, second, first)], axis=1)
    placed = lax.ppermute(sideways, COL, [(i, (i + 1) % N_COL) for i in range(N_COL)])
    rows, cols = block_row.reshape(NNZ), block_col.reshape(NNZ)
    owner = rows >> 1
    side = jnp.where(jnp.arange(NNZ) < tile_count.reshape(1), rows & 1, 2)
    slots = (owner & (N_NEAR - 1)) * N_Z_HI + (owner >> 3) + (side << 6) + (cols << 8)
    at_row = lax.broadcasted_iota(jnp.int32, (PAIR - K, PAIR), 0)
    extra = jnp.where(at_row == K, residual.reshape(1, PAIR), 0.0)
    blocks, slots, extra, sent = lax.optimization_barrier((tangent.reshape(NNZ, BLK, BLK), slots, extra, placed))
    copies = jnp.broadcast_to(sent[None], (N_ROW, K, PAIR))
    col_basis = lax.all_to_all(copies, ROW, 0, 0, tiled=True)
    partial = pl.pallas_call(
        product_kernel,
        out_shape=jax.ShapeDtypeStruct((N_COL, WORDS, PAIR), jnp.int32),
        in_specs=[smem, vmem, vmem],
        out_specs=vmem,
        scratch_shapes=[pltpu.VMEM((2 * N_ROW, K, BLK), jnp.bfloat16), pltpu.VMEM((N_COL, K, PAIR), jnp.float32)],
        compiler_params=params,
    )(slots, blocks, col_basis)
    near = lax.all_to_all(partial, NEAR, 0, 0, tiled=True)
    near = pl.pallas_call(
        near_kernel,
        out_shape=jax.ShapeDtypeStruct((N_Z_HI, WORDS, PAIR), jnp.int32),
        in_specs=[vmem],
        out_specs=vmem,
        scratch_shapes=[pltpu.VMEM((N_NEAR, K, PAIR), jnp.float32), pltpu.VMEM((N_Z_HI, K, PAIR), jnp.float32)],
        compiler_params=params,
    )(near.reshape(N_NEAR, N_Z_HI, WORDS, PAIR))
    far = lax.all_to_all(near, "z_hi", 0, 0, tiled=True)
    product, gram = pl.pallas_call(
        gram_kernel,
        out_shape=(
            jax.ShapeDtypeStruct((K, PAIR), jnp.float32),
            jax.ShapeDtypeStruct((4, 4 * 2 * K), jnp.float32),
        ),
        in_specs=[vmem, vmem],
        out_specs=(vmem, vmem),
        compiler_params=params,
    )(far, extra)
    gram = summed(gram, ("core", "x"), N_CORE * N_X)
    gram = summed(gram, ("z_hi", "z_lo"), N_Z_HI * N_Z_LO)
    gram = summed(gram, "y", N_Y)
    out_c, out_u, coefficients = pl.pallas_call(
        finish_kernel,
        out_shape=(
            jax.ShapeDtypeStruct((2, BLK * K), jnp.bfloat16),
            jax.ShapeDtypeStruct((2, BLK * K), jnp.bfloat16),
            jax.ShapeDtypeStruct((K,), jnp.float32),
        ),
        in_specs=[vmem, vmem, vmem],
        out_specs=(vmem, vmem, vmem),
        scratch_shapes=[pltpu.VMEM((2 * PAIR, PAIR), jnp.float32)],
        compiler_params=params,
    )(gram, product, placed)
    return (out_c, out_u, coefficients)


def solution(mesh):
    split = Mesh(mesh.devices.reshape(N_Y, N_CORE, N_Z_HI, N_Z_LO, N_X), ROW + COL)
    return jax.shard_map(
        per_device,
        mesh=split,
        in_specs=(
            P(ROW, COL, None, None),
            P(ROW, COL, None),
            P(ROW, COL, None),
            P(ROW, COL),
            P(ROW + COL, None),
            P(ROW + COL),
            P(ROW + COL),
        ),
        out_specs=(P(ROW + COL, None), P(ROW + COL, None), P()),
        check_vma=False,
    )
```

```python
import math

import jax
import jax.numpy as jnp
from jax import lax
from jax.experimental import pallas as pl
from jax.experimental.pallas import tpu as pltpu
from jax.sharding import Mesh
from jax.sharding import PartitionSpec as P

BLK = 64
K = 48
PAIR = 2 * BLK
N_X, N_Y, N_CORE = 4, 8, 2
N_Z_HI, N_Z_LO = 8, 2
ROW = ("y", "core")
NEAR = ("z_lo", "x")
COL = ("z_hi",) + NEAR
N_ROW = N_Y * N_CORE
N_NEAR = N_Z_LO * N_X
N_COL = N_Z_HI * N_NEAR
NNZ = 64
TOTAL = N_ROW * N_COL * PAIR
HIGHEST = lax.Precision.HIGHEST
VMEM = 48 * 1024 * 1024


HALF = BLK // 4
PANEL = 8
BATCH = 64
SHIFT = K
INNER = 2 * K
WORDS = 2 * HALF
STEPS = (64, 32, 16, 8, 4, 2, 1)
LOWEST = 100
MAGIC = 12582912.0


def encode(sums_ref, count, out_ref):
    def look(i, peak):
        return jnp.maximum(peak, jnp.abs(sums_ref[i]))

    peak = lax.fori_loop(0, count, look, jnp.zeros((K, PAIR), jnp.float32), unroll=count)
    peak = jnp.broadcast_to(jnp.max(peak, axis=1, keepdims=True), (K, PAIR))
    factor = jnp.full((K, PAIR), 2.0**19, jnp.float32)
    power = jnp.zeros((K, PAIR), jnp.int32)
    for step in STEPS:
        big = peak >= 2.0**step
        peak = jnp.where(big, peak * 2.0**-step, peak)
        factor = jnp.where(big, factor * 2.0**-step, factor)
        power = jnp.where(big, power + step, power)
    for step in STEPS:
        small = (peak < 2.0 ** (1 - step)) & (power - step >= -LOWEST)
        peak = jnp.where(small, peak * 2.0**step, peak)
        factor = jnp.where(small, factor * 2.0**step, factor)
        power = jnp.where(small, power - step, power)
    power = power + LOWEST
    lane = lax.broadcasted_iota(jnp.int32, (HALF, PAIR), 1)
    shown = jnp.where(lane < 8, power[:HALF], jnp.where(lane < 16, power[HALF:WORDS], power[WORDS:]))
    flags = ((shown >> (lane & 7)) & 1) << 10

    def put(i, carry):
        code = ((sums_ref[i] * factor + MAGIC) - MAGIC).astype(jnp.int32)
        code = jnp.minimum(code, (1 << 20) - 1)
        third = code[WORDS:]
        out_ref[i, :HALF] = (code[:HALF] << 11) | ((third >> 10) & 0x7FF)
        out_ref[i, HALF:] = (code[HALF:WORDS] << 11) | (third & 0x3FF) | flags
        return carry

    lax.fori_loop(0, count, put, 0, unroll=count)


def unit_of(second):
    lane = lax.broadcasted_iota(jnp.int32, (HALF, PAIR), 1)
    bits = (((second >> 10) & 1) << (lane & 7)).astype(jnp.float32)
    power = jnp.concatenate(
        [
            jnp.sum(jnp.where((lane >= 8 * i) & (lane < 8 * i + 8), bits, 0.0), axis=1, keepdims=True)
            for i in range(3)
        ],
        axis=0,
    )
    power = jnp.broadcast_to(power, (K, PAIR)).astype(jnp.int32)
    unit = jnp.full((K, PAIR), 2.0 ** (-LOWEST - 19), jnp.float32)
    for i in range(8):
        steps = (2.0 ** (1 << i),) if i < 7 else (2.0**64, 2.0**64)
        for step in steps:
            unit = jnp.where(((power >> i) & 1) == 1, unit * step, unit)
    return unit


def decode(words):
    first, second = words[:HALF], words[HALF:]
    third = ((first << 21) >> 11) | (second & 0x3FF)
    return jnp.concatenate([first >> 11, second >> 11, third], axis=0).astype(jnp.float32)


def near_kernel(near_ref, out_ref, unit_ref, sums_ref):
    for source in range(N_NEAR):
        unit_ref[source] = unit_of(near_ref[source, 0, HALF:])

    for i in range(N_Z_HI):
        total = decode(near_ref[0, i]) * unit_ref[0]
        for source in range(1, N_NEAR):
            total += decode(near_ref[source, i]) * unit_ref[source]
        sums_ref[i] = total
    encode(sums_ref, N_Z_HI, out_ref)


def product_kernel(slot_ref, tangent_ref, basis_ref, out_ref, half_ref, sums_ref):
    for q in range(N_ROW):
        half_ref[2 * q] = basis_ref[q, :, :BLK]
        half_ref[2 * q + 1] = basis_ref[q, :, BLK:]
    sums_ref[...] = jnp.zeros_like(sums_ref)

    side_of_lane = lax.broadcasted_iota(jnp.int32, (K, PAIR), 1) >> 6

    def add_blocks(step, carry):
        places, products = [], []
        for i in range(BATCH):
            n = step * BATCH + i
            slot = slot_ref[n]
            places.append(slot & (N_COL - 1))
            side = (slot >> 6) & 3
            product = lax.dot_general(
                half_ref[slot >> 8], tangent_ref[n], (((1,), (1,)), ((), ())), preferred_element_type=jnp.float32
            )
            products.append(jnp.where(side_of_lane == side, jnp.concatenate([product, product], axis=1), 0.0))
        for place, product in zip(places, products):
            sums_ref[place] += product
        return carry

    lax.fori_loop(0, NNZ // BATCH, add_blocks, 0)
    encode(sums_ref, N_COL, out_ref)


def gram_kernel(far_ref, extra_ref, product_ref, gram_ref):
    product = decode(far_ref[0]) * unit_of(far_ref[0, HALF:])
    for source in range(1, N_Z_HI):
        product += decode(far_ref[source]) * unit_of(far_ref[source, HALF:])
    product_ref[...] = product
    both = jnp.concatenate([product, extra_ref[...]], axis=0)
    gram = lax.dot_general(product, both, (((1,), (1,)), ((), ())), precision=HIGHEST)
    row = lax.broadcasted_iota(jnp.int32, (HALF, PAIR), 0)
    lane = lax.broadcasted_iota(jnp.int32, (HALF, PAIR), 1)

    def by_lane(bottom, middle, top):
        return jnp.where(lane < K, bottom, jnp.where(lane < 80, middle, top))

    top, middle, bottom = gram[:HALF], gram[HALF:WORDS], gram[WORDS:]
    packed = by_lane(bottom, pltpu.roll(middle, K, 1), pltpu.roll(top, 80, 1))
    inner = by_lane(*(jnp.broadcast_to(part[:, INNER : INNER + 1], (HALF, PAIR)) for part in (bottom, middle, top)))
    place = lane - by_lane(32, 64, 80)
    packed = jnp.where(place == row + 1, inner, packed)
    packed = jnp.where((place == 2) & (row == 0), inner[HALF - 1 :], packed)
    gram_ref[...] = jnp.concatenate([packed[i : i + 4, : 2 * K] for i in range(0, HALF, 4)], axis=1)


def finish_kernel(gram_ref, product_ref, basis_ref, out_c_ref, out_u_ref, coeff_ref, both_ref):
    wide = gram_ref[...]
    packed = jnp.concatenate([wide[:, 2 * K * i : 2 * K * (i + 1)] for i in range(4)], axis=0)
    packed = jnp.concatenate([packed, jnp.zeros((HALF, PAIR - 2 * K), jnp.float32)], axis=1)
    blocks = jnp.concatenate([pltpu.roll(packed, K, 1), pltpu.roll(packed, 80, 1), packed], axis=0)
    at_row = lax.broadcasted_iota(jnp.int32, (K, PAIR), 0)
    at_lane = lax.broadcasted_iota(jnp.int32, (K, PAIR), 1)
    inner = jnp.sum(jnp.where(at_lane == at_row + 1, blocks, 0.0), axis=1, keepdims=True)
    last = jnp.sum(jnp.where(at_lane == at_row + 2, blocks, 0.0), axis=1, keepdims=True)
    last = jnp.concatenate([jnp.broadcast_to(last[i : i + 1], (HALF, 1)) for i in range(0, K, HALF)], axis=0)
    inner = jnp.where((at_row & (HALF - 1)) == HALF - 1, last, inner)
    blocks = blocks * (1.0 / TOTAL)
    below = jnp.concatenate([jnp.where(at_lane < at_row, blocks, 0.0), jnp.zeros((PAIR - K, PAIR), jnp.float32)], axis=0)
    work = jnp.where(at_lane <= at_row, blocks, below.T[:K])
    work = jnp.where(at_lane == INNER, inner, work)
    work = jnp.where(at_lane == at_row + SHIFT, 1.0, work)
    groups = [work[i : i + 8] for i in range(0, K, 8)]
    in_group = at_row[:8]
    pivots = [jnp.ones((8, PAIR), jnp.float32)] * len(groups)
    for start in range(0, K, PANEL):
        own = start // 8
        first = start % 8
        columns = [
            [jnp.broadcast_to(group[:, k : k + 1], (8, PAIR)) for group in groups[own:]]
            for k in range(start, start + PANEL)
        ]
        rows = [groups[own][first + i : first + i + 1] for i in range(PANEL)]
        for i in range(PANEL):
            pivot = columns[i][0][first + i : first + i + 1]
            pivots[own] = jnp.where(in_group == first + i, pivot, pivots[own])
            inverse = 1.0 / pivot
            rows[i] = rows[i] * inverse
            for j in range(i + 1, PANEL):
                entry = columns[i][0][first + j : first + j + 1]
                rows[j] = rows[j] - entry * rows[i]
                factor = entry * inverse
                columns[j] = [old - factor * left for old, left in zip(columns[j], columns[i])]
            columns[i][0] = jnp.where(in_group > first + i, columns[i][0], 0.0)
        for g in range(own, len(groups)):
            for i in range(PANEL):
                groups[g] = groups[g] - columns[i][g - own] * rows[i]
    work = jnp.concatenate([group / jnp.sqrt(pivot) for group, pivot in zip(groups, pivots)], axis=0)
    inverse = jnp.where((at_lane >= SHIFT) & (at_lane < INNER), work, 0.0)
    columns = jnp.concatenate([product_ref[...], basis_ref[...].astype(jnp.float32)], axis=1)
    tall = jnp.concatenate(
        [jnp.zeros((SHIFT, 2 * PAIR), jnp.float32), columns, jnp.zeros((PAIR - INNER, 2 * PAIR), jnp.float32)], axis=0
    )
    both_ref[:, :K] = jnp.dot(inverse, tall, precision=HIGHEST).T
    flat = jnp.concatenate([both_ref[pl.ds(j, 32, stride=8), :][:, :K] for j in range(8)], axis=1)
    for j in range(8):
        lanes = slice(8 * K * j, 8 * K * (j + 1))
        out_c_ref[:, lanes] = jnp.concatenate([flat[j : j + 1], flat[8 + j : 9 + j]], axis=0).astype(jnp.bfloat16)
        out_u_ref[:, lanes] = jnp.concatenate([flat[16 + j : 17 + j], flat[24 + j : 25 + j]], axis=0).astype(jnp.bfloat16)
    inner = work[:, INNER : INNER + 1] * (1.0 / math.sqrt(TOTAL))
    coeff_ref[...] = jnp.sum(jnp.where(at_lane == at_row, inner, 0.0), axis=0)[:K]


def summed(array, axes, count):
    copies = jnp.broadcast_to(array[None], (count,) + array.shape)
    return jnp.sum(lax.all_to_all(copies, axes, 0, 0, tiled=True), axis=0)


def per_device(tangent, block_row, block_col, tile_count, old_basis, old_id, residual):
    params = pltpu.CompilerParams(vmem_limit_bytes=VMEM)
    smem = pl.BlockSpec(memory_space=pltpu.SMEM)
    vmem = pl.BlockSpec(memory_space=pltpu.VMEM)
    first, second = (old_basis[i].reshape(BLK, K).T for i in (0, 1))
    kept = old_id[0] % 2 == 0
    sideways = jnp.concatenate([jnp.where(kept, first, second), jnp.where(kept, second, first)], axis=1)
    placed = lax.ppermute(sideways, COL, [(i, (i + 1) % N_COL) for i in range(N_COL)])
    rows, cols = block_row.reshape(NNZ), block_col.reshape(NNZ)
    owner = rows >> 1
    side = jnp.where(jnp.arange(NNZ) < tile_count.reshape(1), rows & 1, 2)
    slots = (owner & (N_NEAR - 1)) * N_Z_HI + (owner >> 3) + (side << 6) + ((((cols >> 1) & 1) * 2 * N_Y + (cols >> 2) * 2 + (cols & 1)) << 8)
    at_row = lax.broadcasted_iota(jnp.int32, (PAIR - K, PAIR), 0)
    extra = jnp.where(at_row == K, residual.reshape(1, PAIR), 0.0)
    blocks, slots, extra, sent = lax.optimization_barrier((tangent.reshape(NNZ, BLK, BLK), slots, extra, placed))
    copies = jnp.broadcast_to(sent[None], (N_ROW, K, PAIR))
    col_basis = lax.all_to_all(copies, ("core", "y"), 0, 0, tiled=True)
    partial = pl.pallas_call(
        product_kernel,
        out_shape=jax.ShapeDtypeStruct((N_COL, WORDS, PAIR), jnp.int32),
        in_specs=[smem, vmem, vmem],
        out_specs=vmem,
        scratch_shapes=[pltpu.VMEM((2 * N_ROW, K, BLK), jnp.bfloat16), pltpu.VMEM((N_COL, K, PAIR), jnp.float32)],
        compiler_params=params,
    )(slots, blocks, col_basis)
    near = lax.all_to_all(partial, NEAR, 0, 0, tiled=True)
    near = pl.pallas_call(
        near_kernel,
        out_shape=jax.ShapeDtypeStruct((N_Z_HI, WORDS, PAIR), jnp.int32),
        in_specs=[vmem],
        out_specs=vmem,
        scratch_shapes=[pltpu.VMEM((N_NEAR, K, PAIR), jnp.float32), pltpu.VMEM((N_Z_HI, K, PAIR), jnp.float32)],
        compiler_params=params,
    )(near.reshape(N_NEAR, N_Z_HI, WORDS, PAIR))
    far = lax.all_to_all(near, "z_hi", 0, 0, tiled=True)
    product, gram = pl.pallas_call(
        gram_kernel,
        out_shape=(
            jax.ShapeDtypeStruct((K, PAIR), jnp.float32),
            jax.ShapeDtypeStruct((4, 4 * 2 * K), jnp.float32),
        ),
        in_specs=[vmem, vmem],
        out_specs=(vmem, vmem),
        compiler_params=params,
    )(far, extra)
    gram = summed(gram, ("core", "x"), N_CORE * N_X)
    gram = summed(gram, ("z_hi", "z_lo"), N_Z_HI * N_Z_LO)
    gram = summed(gram, "y", N_Y)
    out_c, out_u, coefficients = pl.pallas_call(
        finish_kernel,
        out_shape=(
            jax.ShapeDtypeStruct((2, BLK * K), jnp.bfloat16),
            jax.ShapeDtypeStruct((2, BLK * K), jnp.bfloat16),
            jax.ShapeDtypeStruct((K,), jnp.float32),
        ),
        in_specs=[vmem, vmem, vmem],
        out_specs=(vmem, vmem, vmem),
        scratch_shapes=[pltpu.VMEM((2 * PAIR, PAIR), jnp.float32)],
        compiler_params=params,
    )(gram, product, placed)
    return (out_c, out_u, coefficients)


def solution(mesh):
    split = Mesh(mesh.devices.reshape(N_Y, N_CORE, N_Z_HI, N_Z_LO, N_X), ROW + COL)
    return jax.shard_map(
        per_device,
        mesh=split,
        in_specs=(
            P(ROW, COL, None, None),
            P(ROW, COL, None),
            P(ROW, COL, None),
            P(ROW, COL),
            P(ROW + COL, None),
            P(ROW + COL),
            P(ROW + COL),
        ),
        out_specs=(P(ROW + COL, None), P(ROW + COL, None), P()),
        check_vma=False,
    )
```
